32 devices in a mesh: groups: 2 (over y), dp: 8 (over z, x), tensor: 2 (over core).
Axes of the slice: x: 2, y: 2, z: 4, core: 2. Of those that a mesh axis runs over, the one named last changes fastest.
Arguments:
- tokens: bfloat16 [2048, 8192], P(('groups', 'dp'), 'tensor'), parts along dimension 0, may hold values from -4 to 4
- gate_weight_base: bfloat16 [14336, 8192], P('dp', 'tensor'), may hold values from -0.0625 to 0.0625
- up_weight_base: bfloat16 [14336, 8192], P('dp', 'tensor'), may hold values from -0.0625 to 0.0625
- adapter_down_stack: bfloat16 [8, 8192, 128], P('dp', 'tensor'), may hold values from -0.0625 to 0.0625
- adapter_up_stack: bfloat16 [8, 128, 14336], P('dp', 'tensor'), may hold values from -2 to 2
- segment_block_counts: int32 [8], P('groups'), parts along dimension 0, may hold values from 1 to 3, 8 in all
- segment_adapter_ids: int32 [8], P('groups'), parts along dimension 0, may hold values from 0 to 7
- segment_live_rows: int32 [8], P('groups'), parts along dimension 0, may hold values from 1 to 128
Outputs:
- ref_hidden: bfloat16 [14336, 2048], P('dp', ('groups', 'tensor')), parts along dimension 1
- pol_hidden: bfloat16 [14336, 2048], P('dp', ('groups', 'tensor')), parts along dimension 1
- seg_kl: float32 [8], P('groups'), parts along dimension 0
The draws below stay inside these ranges and needn't reach their ends.
There are 2 independent parts, one for each index of `groups`. The reference program is written for one: setup_inputs(seed, part) draws one part's arguments, and reference() takes and returns one part's arrays. A program takes and returns all parts, laid end to end along the dimension named above; an argument that names none is the same for every part. Nothing has to cross between parts.
All inputs are finite; a program needn't handle non-finite values.
Results may differ from the reference program's by a relative error of at most 0.0052.
Values may be sent and summed in bfloat16 or wider, within the bound.
A program may use at most 192 MiB of HBM per device.

```python
import math
import jax
import jax.numpy as jnp
import numpy as np

MODEL_WIDTH = 8192
HIDDEN_UNITS = 14336
ADAPTER_RANK = 64
BLOCK = 128
ROWS = 1024
ADAPTER_COUNT = 8
BLOCKS = 8
SEGS = 4
MOSTB = 3


def draw_tokens(key, part):
    key = jax.random.fold_in(key, 11)
    shared_key, row_key = jax.random.split(key)
    shared = jax.random.normal(shared_key, (1, MODEL_WIDTH), jnp.float32)
    private = jax.random.normal(row_key, (ROWS, MODEL_WIDTH), jnp.float32)
    blended = 0.8 * shared + 0.6 * private
    return jnp.clip(blended, -4.0, 4.0).astype(jnp.bfloat16)


def draw_adapter_up_stack(key, part):
    key = jax.random.fold_in(key, 23)
    scale_key, entry_key = jax.random.split(key)
    spread = jax.random.uniform(scale_key, (ADAPTER_COUNT, 1, HIDDEN_UNITS), jnp.float32, 1.0 / 256.0, 1.0)
    column_scale = 0.25 * spread ** (-0.5)
    entries = jax.random.normal(entry_key, (ADAPTER_COUNT, 2 * ADAPTER_RANK, HIDDEN_UNITS), jnp.float32)
    scaled = entries * column_scale * (1.0 / math.sqrt(ADAPTER_RANK))
    return jnp.clip(scaled, -2.0, 2.0).astype(jnp.bfloat16)


def with_ends(values, key, low, high):
    longest = values.shape.index(max(values.shape))
    spots = []
    for shift in (0, 1):
        where = [jax.random.randint(jax.random.fold_in(key, axis), (), 0, length) for axis, length in enumerate(values.shape)]
        where[longest] = (where[longest] + shift) % values.shape[longest]
        spots.append(tuple(where))
    return values.at[spots[0]].set(low).at[spots[1]].set(high)


def levels(key, shape, shards, least, high):
    def one(position, parts):
        draws = jax.random.uniform(jax.random.fold_in(jax.random.fold_in(key, 6), position), (parts,), jnp.float32, least / len(shards), high / len(shards))
        return jnp.repeat(jnp.exp(draws), shape[position] // parts).reshape((-1,) + (1,) * (len(shape) - position - 1))

    level = one(*shards[0])
    for cut in shards[1:]:
        level = level * one(*cut)
    return level


def rank_bounds(count, lean):
    weights = [(1 << 20) // math.isqrt(rank ** lean) + 1 for rank in range(1, count + 1)]
    width = 1 + sum(weights) // (1 << 30)
    return np.cumsum(np.array([max(1, weight // width) for weight in weights]))


def skewed_ids(own_key, dims, count, skew):
    listing = rank_bounds(count, skew)
    pick = jax.random.randint(jax.random.fold_in(own_key, 1), dims, 0, int(listing[count - 1]))
    grade = jnp.searchsorted(jnp.asarray(listing, jnp.int32), pick, side="right")
    return jax.random.permutation(jax.random.fold_in(own_key, 2), count)[grade].astype(jnp.int32)


def length_profile(number_of, total, bound, skew):
    portions = [(1 << 20) // math.isqrt(standing ** skew) + 1 for standing in range(2, number_of + 1)]
    surplus, given = total - bound - (number_of - 1), [1] * (number_of - 1)
    while surplus > 0:
        free = [i for i in range(number_of - 1) if given[i] < bound]
        mass, left = sum([portions[i] for i in free]), surplus
        for i in free:
            addition = min(bound - given[i], max(1, left * portions[i] // mass), surplus)
            given[i] = given[i] + addition
            surplus = surplus - addition
    return np.array([bound] + given)


def uneven(stream_key, count, total, reach, slope):
    if count == 2:
        one = jax.random.randint(stream_key, (), max(1, total - reach), min(reach, total - 1) + 1)
        return jnp.stack([one, total - one])
    sizes = jnp.asarray(length_profile(count, total, reach, slope), jnp.int32)
    pairs = (count - 1) // 2
    giver, receiver = sizes[1:1 + 2 * pairs:2], sizes[2:2 + 2 * pairs:2]
    margin = jnp.minimum(giver - 1, reach - receiver)
    moved = jax.random.randint(jax.random.fold_in(stream_key, 1), (pairs,), 0, 1 << 20) % (margin + 1)
    sizes = sizes.at[1:1 + 2 * pairs:2].set(giver - moved).at[2:2 + 2 * pairs:2].set(receiver + moved)
    return sizes[jax.random.permutation(jax.random.fold_in(stream_key, 2), count)]


def gaussian(stream_key, extent, width, most, shards=(), kind=jnp.bfloat16):
    values = jax.random.normal(stream_key, extent, jnp.float32) * width
    if len(shards) > 0:
        values = levels(stream_key, extent, shards, -0.22, 0.18) * values
    return jnp.clip(values, min=-most, max=most).astype(kind)


def setup_inputs(seed: int = 0, part: int = 0) -> dict:
    key_of = jax.random.split(jax.random.key(seed), 9)
    part_keys = jax.random.split(jax.random.fold_in(key_of[8], part), 9)
    tokens = draw_tokens(jax.random.fold_in(jax.random.fold_in(key_of[8], part), 71), part)
    gate_weight_base = gaussian(key_of[1], (HIDDEN_UNITS, MODEL_WIDTH), MODEL_WIDTH ** -0.5, 0.0625, ((0, 8), (1, 2)))
    up_weight_base = gaussian(key_of[2], (HIDDEN_UNITS, MODEL_WIDTH), MODEL_WIDTH ** -0.5, 0.0625, ((0, 8), (1, 2)))
    adapter_down_stack = gaussian(key_of[3], (ADAPTER_COUNT, MODEL_WIDTH, 2 * ADAPTER_RANK), MODEL_WIDTH ** -0.5, 0.0625, ((0, 8), (1, 2)))
    adapter_up_stack = draw_adapter_up_stack(jax.random.fold_in(key_of[8], 71), part)
    segment_block_counts = uneven(part_keys[5], SEGS, BLOCKS, MOSTB, 2).astype(jnp.int32)
    segment_adapter_ids = with_ends(skewed_ids(part_keys[6], (SEGS,), ADAPTER_COUNT, 2), jax.random.fold_in(part_keys[6], 3), 0, ADAPTER_COUNT - 1).astype(jnp.int32)
    segment_live_rows = with_ends(jax.random.randint(part_keys[7], (SEGS,), 1, BLOCK + 1), jax.random.fold_in(part_keys[7], 1), 1, BLOCK).astype(jnp.int32)
    return {"tokens": tokens, "gate_weight_base": gate_weight_base, "up_weight_base": up_weight_base, "adapter_down_stack": adapter_down_stack, "adapter_up_stack": adapter_up_stack, "segment_block_counts": segment_block_counts, "segment_adapter_ids": segment_adapter_ids, "segment_live_rows": segment_live_rows}


def segment_tables(segment_block_counts, segment_live_rows, total_rows):
    seg_ends = jnp.cumsum(segment_block_counts).astype(jnp.int32)
    starts = (seg_ends - segment_block_counts).astype(jnp.int32)
    row_ids = jnp.arange(total_rows, dtype=jnp.int32)
    blocks = row_ids // BLOCK
    member = (blocks[None, :] >= starts[:, None]) & (blocks[None, :] < seg_ends[:, None])
    live_limit = (seg_ends - 1) * BLOCK + segment_live_rows
    live_rows = member & (row_ids[None, :] < live_limit[:, None])
    counts = (live_limit - starts * BLOCK).astype(jnp.float32)
    return member, live_rows, counts


def reference(tokens, gate_weight_base, up_weight_base, adapter_down_stack, adapter_up_stack, segment_block_counts, segment_adapter_ids, segment_live_rows):
    member, live_rows, counts = segment_tables(segment_block_counts, segment_live_rows, ROWS)
    weights = member.astype(jnp.float32)
    gate_ref = jnp.dot(tokens, gate_weight_base.T, preferred_element_type=jnp.float32)
    up_ref = jnp.dot(tokens, up_weight_base.T, preferred_element_type=jnp.float32)
    down_sum = jnp.zeros((ROWS, 2 * ADAPTER_RANK), jnp.float32)
    for buffer_slot in range(SEGS):
        down_weight_matrix = adapter_down_stack[segment_adapter_ids[buffer_slot]]
        down_sum = down_sum + weights[buffer_slot][:, None] * jnp.dot(tokens, down_weight_matrix, preferred_element_type=jnp.float32)
    down_proj = down_sum.astype(jnp.bfloat16)
    gate_pol = gate_ref
    up_pol = up_ref
    for buffer_slot in range(SEGS):
        up_weight_matrix = adapter_up_stack[segment_adapter_ids[buffer_slot]]
        gate_pol = gate_pol + weights[buffer_slot][:, None] * jnp.dot(down_proj[:, :ADAPTER_RANK], up_weight_matrix[:ADAPTER_RANK], preferred_element_type=jnp.float32)
        up_pol = up_pol + weights[buffer_slot][:, None] * jnp.dot(down_proj[:, ADAPTER_RANK:], up_weight_matrix[ADAPTER_RANK:], preferred_element_type=jnp.float32)
    ref_hidden = (jax.nn.silu(gate_ref) * up_ref).astype(jnp.bfloat16)
    pol_hidden = (jax.nn.silu(gate_pol) * up_pol).astype(jnp.bfloat16)
    ref_vals = 4.0 * jnp.tanh(ref_hidden.astype(jnp.float32) * 0.25)
    pol_vals = 4.0 * jnp.tanh(pol_hidden.astype(jnp.float32) * 0.25)
    pol_exp = jnp.exp(pol_vals)
    ref_sum = jnp.sum(jnp.exp(ref_vals), axis=1)
    pol_sum = jnp.sum(pol_exp, axis=1)
    cross_sum = jnp.sum(pol_exp * (pol_vals - ref_vals), axis=1)
    kl_row = cross_sum / pol_sum - jnp.log(pol_sum) + jnp.log(ref_sum)
    seg_kl = jnp.sum(live_rows.astype(jnp.float32) * kl_row[None, :], axis=1) / counts
    return ref_hidden.T, pol_hidden.T, seg_kl
```

```python
import functools
import jax
import jax.numpy as jnp
from jax import lax
from jax.experimental import pallas as pl
from jax.experimental.pallas import tpu as pltpu
from jax.sharding import PartitionSpec as P

BLOCK = 128


def spread_2(value, axis, root):
    mine = lax.axis_index(axis) == root
    return lax.psum(jnp.where(mine, value, jnp.zeros_like(value)), axis)


def segment_tables(segment_block_counts, segment_live_rows, total_rows):
    seg_ends = jnp.cumsum(segment_block_counts)
    starts = seg_ends - segment_block_counts
    row_ids = jnp.arange(total_rows, dtype=jnp.int32)
    blocks = row_ids // BLOCK
    member = (blocks[None, :] >= starts[:, None]) & (blocks[None, :] < seg_ends[:, None])
    live_limit = (seg_ends - 1) * BLOCK + segment_live_rows
    live_rows = member & (row_ids[None, :] < live_limit[:, None])
    counts = (live_limit - starts * BLOCK).astype(jnp.float32)
    return (member, live_rows, counts)


def project_tokens(tokens, gate_weight_base, up_weight_base, adapter_down_matrix, owned_rows):
    contract = (((1,), (1,)), ((), ()))
    rank_pair = adapter_down_matrix.shape[1]
    block_rows = lax.all_gather(tokens, "dp", axis=0, tiled=True)
    row_count = block_rows.shape[0]
    gate_part = lax.dot_general(
        gate_weight_base, block_rows, contract, preferred_element_type=jnp.float32
    )
    up_part = lax.dot_general(
        up_weight_base, block_rows, contract, preferred_element_type=jnp.float32
    )
    base_terms = jnp.stack([gate_part, up_part])
    contrib = lax.cond(
        jnp.any(owned_rows),
        lambda: jnp.dot(block_rows, adapter_down_matrix, preferred_element_type=jnp.float32)
        * owned_rows[:, None].astype(jnp.float32),
        lambda: jnp.zeros((row_count, rank_pair), jnp.float32),
    )
    return (base_terms, contrib)


def shards(
    tokens,
    gate_weight_base,
    up_weight_base,
    adapter_down_stack,
    adapter_up_stack,
    segment_block_counts,
    segment_adapter_ids,
    segment_live_rows,
):
    dp_count = lax.axis_size("dp")
    tp_count = lax.axis_size("tensor")
    dp_index = lax.axis_index("dp")
    tp_index = lax.axis_index("tensor")
    local_rows = tokens.shape[0]
    total_rows = local_rows * dp_count
    rows_half = total_rows // tp_count
    seg_count = segment_block_counts.shape[0]
    member, live_rows, counts = segment_tables(segment_block_counts, segment_live_rows, total_rows)
    adapter_down_matrix = adapter_down_stack[0]
    rank_pair = adapter_down_matrix.shape[1]
    base_terms, unused_terms = project_tokens(
        tokens,
        gate_weight_base,
        up_weight_base,
        adapter_down_matrix,
        jnp.zeros((total_rows,), jnp.bool_),
    )
    home_first = dp_index * local_rows
    home_member = lax.dynamic_slice_in_dim(member, home_first, local_rows, 1).astype(jnp.float32)

    def fetch_slot(buffer_slot, accum):
        fetched = spread_2(adapter_down_matrix, "dp", segment_adapter_ids[buffer_slot])
        return (
            accum
            + jnp.dot(tokens, fetched, preferred_element_type=jnp.float32)
            * home_member[buffer_slot][:, None]
        )

    home_terms = lax.fori_loop(
        0, seg_count, fetch_slot, jnp.zeros((local_rows, rank_pair), jnp.float32)
    )
    down_terms = lax.dynamic_update_slice_in_dim(
        jnp.zeros((total_rows, rank_pair), jnp.float32), home_terms, home_first, 0
    )
    down_proj = lax.psum(down_terms, ("dp", "tensor")).astype(jnp.bfloat16)
    slice_list = lax.all_to_all(adapter_up_stack, "dp", split_axis=2, concat_axis=0, tiled=True)
    adapters = slice_list.shape[0]
    rank_part = slice_list.shape[1]
    ff_dev = slice_list.shape[2]
    picker = (
        segment_adapter_ids[:, None] == jnp.arange(adapters, dtype=jnp.int32)[None, :]
    ).astype(jnp.bfloat16)
    chosen = jnp.einsum(
        "sa,aqf->sqf", picker, slice_list, preferred_element_type=jnp.float32
    ).astype(jnp.bfloat16)
    own_ranks = lax.dynamic_slice_in_dim(down_proj, tp_index * rank_part, rank_part, 1)
    spread = (member.T.astype(jnp.bfloat16)[:, :, None] * own_ranks[:, None, :]).reshape(
        total_rows, seg_count * rank_part
    )
    delta_cols = lax.dot_general(
        chosen.reshape(seg_count * rank_part, ff_dev),
        spread,
        (((0,), (1,)), ((), ())),
        preferred_element_type=jnp.float32,
    )
    upper = tp_index >= tp_count // 2
    blank = jnp.zeros_like(delta_cols)
    policy_terms = base_terms + jnp.stack(
        [jnp.where(upper, blank, delta_cols), jnp.where(upper, delta_cols, blank)]
    )
    halves = lax.psum_scatter(
        jnp.stack([base_terms, policy_terms]), "tensor", scatter_dimension=3, tiled=True
    )
    ref_hidden = (jax.nn.silu(halves[0, 0]) * halves[0, 1]).astype(jnp.bfloat16)
    pol_hidden = (jax.nn.silu(halves[1, 0]) * halves[1, 1]).astype(jnp.bfloat16)
    ref_vals = 4.0 * jnp.tanh(ref_hidden.astype(jnp.float32) * 0.25)
    pol_vals = 4.0 * jnp.tanh(pol_hidden.astype(jnp.float32) * 0.25)
    pol_exp = jnp.exp(pol_vals)
    first_half = tp_index * rows_half

    def placed(values):
        return lax.dynamic_update_slice_in_dim(
            jnp.zeros((total_rows,), jnp.float32), values, first_half, 0
        )

    ref_sum, pol_sum, cross_sum = lax.psum(
        (
            placed(jnp.sum(jnp.exp(ref_vals), axis=0)),
            placed(jnp.sum(pol_exp, axis=0)),
            placed(jnp.sum(pol_exp * (pol_vals - ref_vals), axis=0)),
        ),
        ("dp", "tensor"),
    )
    kl_row = cross_sum / pol_sum - jnp.log(pol_sum) + jnp.log(ref_sum)
    seg_kl = jnp.sum(live_rows.astype(jnp.float32) * kl_row[None, :], axis=1) / counts
    return (ref_hidden, pol_hidden, seg_kl)


MESH = pl.DeviceIdType.MESH


def ring_place(dp_index, count):
    odd = dp_index % 2
    return odd * (count - 1 - dp_index // 2) + (1 - odd) * (dp_index // 2)


def ring_index(place, count):
    upper = place // (count // 2)
    return (1 - upper) * 2 * place + upper * (2 * (count - 1 - place) + 1)


def gather_project(
    dp_count, tp_count, group_count, unit_chunk,
    tokens, gate, up, down, adapter_up,
    own_out, peer_out, adapters_out, contrib_out,
    tok_buf, weights, down_buf, parts, contrib,
    load_sem, ring_send, ring_recv, ad_send, ad_recv, pass_send, pass_recv,
    part_send, part_recv, out_sem,
):
    half = dp_count // 2
    rows = tokens.shape[0]
    units = gate.shape[0]
    ranks = adapter_up.shape[0]
    me = lax.axis_index("dp")
    core = lax.axis_index("tensor")
    group = lax.axis_index("groups")
    place = ring_place(me, dp_count)
    right = ring_index((place + 1) % dp_count, dp_count)
    left = ring_index((place + dp_count - 1) % dp_count, dp_count)
    other_core = 1 - core
    other_group = 1 - group

    barrier = pltpu.get_barrier_semaphore()
    for k in range(1, dp_count):
        pl.semaphore_signal(barrier, inc=1, device_id={"dp": (me + k) % dp_count}, device_id_type=MESH)
    pl.semaphore_signal(barrier, inc=1, device_id={"tensor": other_core}, device_id_type=MESH)
    pl.semaphore_signal(barrier, inc=1, device_id={"groups": other_group}, device_id_type=MESH)
    pl.semaphore_wait(barrier, dp_count + 1)

    def block(slot):
        return tok_buf.at[pl.ds(slot * rows, rows)]

    def send(src, dst, sem, axis, target, sends, recvs):
        copy = pltpu.make_async_remote_copy(
            src_ref=src, dst_ref=dst, send_sem=sends.at[sem], recv_sem=recvs.at[sem],
            device_id={axis: target}, device_id_type=MESH,
        )
        copy.start()
        return copy

    last = dp_count - 1
    cut = rows // 2
    cw = send(tokens, block(1), 0, "dp", right, ring_send, ring_recv)
    ccw = send(tokens, block(2), 1, "dp", left, ring_send, ring_recv)

    loads = [
        pltpu.make_async_copy(tokens, block(0), load_sem.at[0]),
        pltpu.make_async_copy(gate, weights.at[0], load_sem.at[1]),
        pltpu.make_async_copy(up, weights.at[1], load_sem.at[2]),
        pltpu.make_async_copy(down, down_buf, load_sem.at[3]),
    ]
    for load in loads:
        load.start()

    share = ranks // group_count
    mine = pl.ds(pl.multiple_of(group * share, 16), share)
    landing = pl.ds(pl.multiple_of(core * ranks + group * share, 16), share)
    ad_copies = []
    for k in range(1, dp_count):
        target = (me + k) % dp_count
        ad_copies.append(send(
            adapter_up.at[mine, pl.ds(pl.multiple_of(target * units, 128), units)],
            adapters_out.at[me, landing], k, "dp", target, ad_send, ad_recv,
        ))
    ad_local = pltpu.make_async_copy(
        adapter_up.at[mine, pl.ds(pl.multiple_of(me * units, 128), units)],
        adapters_out.at[me, landing], load_sem.at[4],
    )
    ad_local.start()
    for load in loads:
        load.wait()

    def project(slot, blocks):
        def chunk(step, carry):
            which = step // (units // unit_chunk)
            first = pl.multiple_of((step % (units // unit_chunk)) * unit_chunk, unit_chunk)
            value = lax.dot_general(
                weights[which, pl.ds(first, unit_chunk), :],
                tok_buf[pl.ds(slot * rows, blocks * rows), :],
                (((1,), (1,)), ((), ())), preferred_element_type=jnp.float32,
            )
            for b in range(blocks):
                parts[slot + b, which, pl.ds(first, unit_chunk), :] = value[:, b * rows:(b + 1) * rows]
            return carry

        contrib[pl.ds(slot * rows, blocks * rows), :] = jnp.dot(
            tok_buf[pl.ds(slot * rows, blocks * rows), :], down_buf[...],
            preferred_element_type=jnp.float32,
        )
        lax.fori_loop(0, 2 * (units // unit_chunk), chunk, 0)

    per_core = dp_count // tp_count
    slot_place = [place]
    for s in range(1, half):
        slot_place += [(place + dp_count - s) % dp_count, (place + s) % dp_count]
    slot_place.append((place + half) % dp_count)
    slot_block = [ring_index(q, dp_count) for q in slot_place]

    def part_copy(slot):
        where = slot_block[slot] % per_core
        return pltpu.make_async_remote_copy(
            src_ref=parts.at[slot], dst_ref=peer_out.at[where],
            send_sem=part_send.at[slot], recv_sem=part_recv.at[where],
            device_id={"tensor": other_core}, device_id_type=MESH,
        )

    def own_copy(slot):
        where = slot_block[slot] % per_core
        return pltpu.make_async_copy(parts.at[slot], own_out.at[where], part_send.at[slot])

    def contrib_copy(slot):
        first = pl.multiple_of(slot_block[slot] * rows, rows)
        return pltpu.make_async_copy(
            contrib.at[pl.ds(slot * rows, rows)], contrib_out.at[pl.ds(first, rows)], out_sem.at[slot]
        )

    def hand_over(slot):
        contrib_copy(slot).start()

        @pl.when(slot_block[slot] // per_core == core)
        def _():
            own_copy(slot).start()

        @pl.when(slot_block[slot] // per_core != core)
        def _():
            part_copy(slot).start()

    project(0, 1)
    hand_over(0)
    sent = [cw, ccw]
    passes = []
    for s in range(1, half):
        cw.wait_recv()
        ccw.wait_recv()
        if s < half - 1:
            cw = send(block(2 * s - 1), block(2 * s + 1), 2 * s, "dp", right, ring_send, ring_recv)
            ccw = send(block(2 * s), block(2 * s + 2), 2 * s + 1, "dp", left, ring_send, ring_recv)
        else:
            a, b = (2 * s - 1) * rows, 2 * s * rows + cut
            z = last * rows
            cw = send(tok_buf.at[pl.ds(a, cut)], tok_buf.at[pl.ds(z, cut)],
                      2 * s, "dp", right, ring_send, ring_recv)
            ccw = send(tok_buf.at[pl.ds(b, cut)], tok_buf.at[pl.ds(z + cut, cut)],
                       2 * s + 1, "dp", left, ring_send, ring_recv)
        sent += [cw, ccw]
        project(2 * s - 1, 2)
        hand_over(2 * s - 1)
        hand_over(2 * s)
        if s == half - 2:
            for copy in ad_copies:
                copy.wait_recv()
            ad_local.wait()
            region = adapters_out.at[:, landing]
            passes.append(send(region, region, 0, "groups", other_group, pass_send, pass_recv))
        if s == half - 1:
            passes[0].wait_recv()
            region = adapters_out.at[:, pl.ds(pl.multiple_of(core * ranks, 16), ranks)]
            passes.append(send(region, region, 1, "tensor", other_core, pass_send, pass_recv))
    cw.wait_recv()
    ccw.wait_recv()
    project(last, 1)
    hand_over(last)

    for copy in sent + ad_copies + passes:
        copy.wait_send()
    passes[1].wait_recv()
    for slot in range(dp_count):
        contrib_copy(slot).wait()

        @pl.when(slot_block[slot] // per_core == core)
        def _():
            own_copy(slot).wait()

        @pl.when(slot_block[slot] // per_core != core)
        def _():
            part_copy(slot).wait_send()

    for where in range(per_core):
        pltpu.make_async_remote_copy(
            src_ref=parts.at[where], dst_ref=peer_out.at[where],
            send_sem=part_send.at[where], recv_sem=part_recv.at[where],
            device_id={"tensor": other_core}, device_id_type=MESH,
        ).wait_recv()


def finish(ids, own, peer, adapters, down_proj, ref_out, pol_out, sums):
    blocks = own.shape[0]
    rows = own.shape[3]
    ranks = down_proj.shape[1] // 2

    @pl.when(pl.program_id(0) == 0)
    def _():
        sums[...] = jnp.zeros_like(sums)

    def silu(v):
        return v / (1.0 + jnp.exp(-v))

    contract = (((0,), (1,)), ((), ()))
    for j in range(blocks):
        columns = slice(j * rows, (j + 1) * rows)
        gate = own[j, 0] + peer[j, 0]
        up = own[j, 1] + peer[j, 1]
        chosen = adapters[ids[j]]
        ref_hidden = (silu(gate) * up).astype(jnp.bfloat16)
        ref_out[:, columns] = ref_hidden
        gate = gate + lax.dot_general(
            chosen[:ranks], down_proj[columns, :ranks], contract, preferred_element_type=jnp.float32
        )
        up = up + lax.dot_general(
            chosen[ranks:], down_proj[columns, ranks:], contract, preferred_element_type=jnp.float32
        )
        pol_hidden = (silu(gate) * up).astype(jnp.bfloat16)
        pol_out[:, columns] = pol_hidden
        ref_vals = 4.0 * jnp.tanh(ref_hidden.astype(jnp.float32) * 0.25)
        pol_vals = 4.0 * jnp.tanh(pol_hidden.astype(jnp.float32) * 0.25)
        pol_exp = jnp.exp(pol_vals)
        for k, value in enumerate((jnp.exp(ref_vals), pol_exp, pol_exp * (pol_vals - ref_vals))):
            sums[k, :, columns] += value.reshape(-1, 8, rows).sum(axis=0)


def kernel_shards(
    tokens, gate_weight_base, up_weight_base, adapter_down_stack, adapter_up_stack,
    segment_block_counts, segment_adapter_ids, segment_live_rows,
):
    dp_count = lax.axis_size("dp")
    tp_count = lax.axis_size("tensor")
    group_count = lax.axis_size("groups")
    dp_index = lax.axis_index("dp")
    tp_index = lax.axis_index("tensor")
    local_rows, features = tokens.shape
    units = gate_weight_base.shape[0]
    ranks = adapter_up_stack.shape[1]
    total_rows = local_rows * dp_count
    per_core = dp_count // tp_count
    rows_half = total_rows // tp_count
    member, live_rows, counts = segment_tables(segment_block_counts, segment_live_rows, total_rows)
    row_adapter = jnp.sum(member.astype(jnp.int32) * segment_adapter_ids[:, None], axis=0)
    f32, bf16 = jnp.float32, jnp.bfloat16
    any_spec = pl.BlockSpec(memory_space=pl.ANY)
    dma = pltpu.SemaphoreType.DMA
    own, peer, adapters, contrib = pl.pallas_call(
        functools.partial(gather_project, dp_count, tp_count, group_count, units // 2),
        out_shape=(
            jax.ShapeDtypeStruct((per_core, 2, units, local_rows), f32),
            jax.ShapeDtypeStruct((per_core, 2, units, local_rows), f32),
            jax.ShapeDtypeStruct((dp_count, tp_count * ranks, units), bf16),
            jax.ShapeDtypeStruct((total_rows, tp_count * ranks), f32),
        ),
        in_specs=[any_spec] * 5,
        out_specs=(any_spec,) * 4,
        scratch_shapes=[
            pltpu.VMEM((total_rows, features), bf16),
            pltpu.VMEM((2, units, features), bf16),
            pltpu.VMEM((features, tp_count * ranks), bf16),
            pltpu.VMEM((dp_count, 2, units, local_rows), f32),
            pltpu.VMEM((total_rows, tp_count * ranks), f32),
            dma((5,)), dma((dp_count,)), dma((dp_count,)), dma((dp_count,)), dma((dp_count,)),
            dma((2,)), dma((2,)), dma((dp_count,)), dma((per_core,)), dma((dp_count,)),
        ],
        compiler_params=pltpu.CompilerParams(
            collective_id=0, has_side_effects=True, vmem_limit_bytes=60 * 1024 * 1024
        ),
        name="gather_project",
    )(tokens, gate_weight_base, up_weight_base, adapter_down_stack[0], adapter_up_stack[0])
    masked = jnp.where((row_adapter == dp_index)[:, None], contrib, 0.0)
    down_proj = lax.psum(masked, ("dp", "tensor")).astype(bf16)
    own_down = lax.dynamic_slice_in_dim(down_proj, tp_index * rows_half, rows_half, 0)
    own_ids = lax.dynamic_slice_in_dim(row_adapter[::local_rows], tp_index * per_core, per_core, 0)
    chunk = 256
    ref_hidden, pol_hidden, sums = pl.pallas_call(
        finish,
        out_shape=(
            jax.ShapeDtypeStruct((units, rows_half), bf16),
            jax.ShapeDtypeStruct((units, rows_half), bf16),
            jax.ShapeDtypeStruct((3, 8, rows_half), f32),
        ),
        grid_spec=pltpu.PrefetchScalarGridSpec(
            num_scalar_prefetch=1,
            grid=(units // chunk,),
            in_specs=[
                pl.BlockSpec((per_core, 2, chunk, local_rows), lambda u, ids: (0, 0, u, 0)),
                pl.BlockSpec((per_core, 2, chunk, local_rows), lambda u, ids: (0, 0, u, 0)),
                pl.BlockSpec((dp_count, tp_count * ranks, chunk), lambda u, ids: (0, 0, u)),
                pl.BlockSpec((rows_half, tp_count * ranks), lambda u, ids: (0, 0)),
            ],
            out_specs=[
                pl.BlockSpec((chunk, rows_half), lambda u, ids: (u, 0)),
                pl.BlockSpec((chunk, rows_half), lambda u, ids: (u, 0)),
                pl.BlockSpec((3, 8, rows_half), lambda u, ids: (0, 0, 0)),
            ],
        ),
        compiler_params=pltpu.CompilerParams(vmem_limit_bytes=40 * 1024 * 1024),
        name="finish",
    )(own_ids, own, peer, adapters, own_down)
    placed = lax.dynamic_update_slice_in_dim(
        jnp.zeros((3, total_rows), f32), sums.sum(axis=1), tp_index * rows_half, 1
    )
    ref_sum, pol_sum, cross_sum = lax.psum(placed, ("dp", "tensor"))
    kl_row = cross_sum / pol_sum - jnp.log(pol_sum) + jnp.log(ref_sum)
    seg_kl = jnp.sum(live_rows.astype(f32) * kl_row[None, :], axis=1) / counts
    return (ref_hidden, pol_hidden, seg_kl)


def pick_shards(*args):
    rows = args[0].shape[0]
    units = args[1].shape[0]
    sizes = (lax.axis_size("groups"), lax.axis_size("tensor"))
    fits = rows == BLOCK and units % 256 == 0 and sizes == (2, 2) and lax.axis_size("dp") % 4 == 0
    return kernel_shards(*args) if fits else shards(*args)


def solution(mesh):
    in_specs = (
        P(("groups", "dp"), "tensor"),
        P("dp", "tensor"),
        P("dp", "tensor"),
        P("dp", "tensor", None),
        P("dp", "tensor", None),
        P("groups"),
        P("groups"),
        P("groups"),
    )
    out_specs = (P("dp", ("groups", "tensor")), P("dp", ("groups", "tensor")), P("groups"))
    return jax.shard_map(pick_shards, mesh=mesh, in_specs=in_specs, out_specs=out_specs, check_vma=False)
```

```python
import functools
import jax
import jax.numpy as jnp
from jax import lax
from jax.experimental import pallas as pl
from jax.experimental.pallas import tpu as pltpu
from jax.sharding import PartitionSpec as P

BLOCK = 128


def spread_2(value, axis, root):
    mine = lax.axis_index(axis) == root
    return lax.psum(jnp.where(mine, value, jnp.zeros_like(value)), axis)


def segment_tables(segment_block_counts, segment_live_rows, total_rows):
    seg_ends = jnp.cumsum(segment_block_counts)
    starts = seg_ends - segment_block_counts
    row_ids = jnp.arange(total_rows, dtype=jnp.int32)
    blocks = row_ids // BLOCK
    member = (blocks[None, :] >= starts[:, None]) & (blocks[None, :] < seg_ends[:, None])
    live_limit = (seg_ends - 1) * BLOCK + segment_live_rows
    live_rows = member & (row_ids[None, :] < live_limit[:, None])
    counts = (live_limit - starts * BLOCK).astype(jnp.float32)
    return (member, live_rows, counts)


def project_tokens(tokens, gate_weight_base, up_weight_base, adapter_down_matrix, owned_rows):
    contract = (((1,), (1,)), ((), ()))
    rank_pair = adapter_down_matrix.shape[1]
    block_rows = lax.all_gather(tokens, "dp", axis=0, tiled=True)
    row_count = block_rows.shape[0]
    gate_part = lax.dot_general(
        gate_weight_base, block_rows, contract, preferred_element_type=jnp.float32
    )
    up_part = lax.dot_general(
        up_weight_base, block_rows, contract, preferred_element_type=jnp.float32
    )
    base_terms = jnp.stack([gate_part, up_part])
    contrib = lax.cond(
        jnp.any(owned_rows),
        lambda: jnp.dot(block_rows, adapter_down_matrix, preferred_element_type=jnp.float32)
        * owned_rows[:, None].astype(jnp.float32),
        lambda: jnp.zeros((row_count, rank_pair), jnp.float32),
    )
    return (base_terms, contrib)


def shards(
    tokens,
    gate_weight_base,
    up_weight_base,
    adapter_down_stack,
    adapter_up_stack,
    segment_block_counts,
    segment_adapter_ids,
    segment_live_rows,
):
    dp_count = lax.axis_size("dp")
    tp_count = lax.axis_size("tensor")
    dp_index = lax.axis_index("dp")
    tp_index = lax.axis_index("tensor")
    local_rows = tokens.shape[0]
    total_rows = local_rows * dp_count
    rows_half = total_rows // tp_count
    seg_count = segment_block_counts.shape[0]
    member, live_rows, counts = segment_tables(segment_block_counts, segment_live_rows, total_rows)
    adapter_down_matrix = adapter_down_stack[0]
    rank_pair = adapter_down_matrix.shape[1]
    base_terms, unused_terms = project_tokens(
        tokens,
        gate_weight_base,
        up_weight_base,
        adapter_down_matrix,
        jnp.zeros((total_rows,), jnp.bool_),
    )
    home_first = dp_index * local_rows
    home_member = lax.dynamic_slice_in_dim(member, home_first, local_rows, 1).astype(jnp.float32)

    def fetch_slot(buffer_slot, accum):
        fetched = spread_2(adapter_down_matrix, "dp", segment_adapter_ids[buffer_slot])
        return (
            accum
            + jnp.dot(tokens, fetched, preferred_element_type=jnp.float32)
            * home_member[buffer_slot][:, None]
        )

    home_terms = lax.fori_loop(
        0, seg_count, fetch_slot, jnp.zeros((local_rows, rank_pair), jnp.float32)
    )
    down_terms = lax.dynamic_update_slice_in_dim(
        jnp.zeros((total_rows, rank_pair), jnp.float32), home_terms, home_first, 0
    )
    down_proj = lax.psum(down_terms, ("dp", "tensor")).astype(jnp.bfloat16)
    slice_list = lax.all_to_all(adapter_up_stack, "dp", split_axis=2, concat_axis=0, tiled=True)
    adapters = slice_list.shape[0]
    rank_part = slice_list.shape[1]
    ff_dev = slice_list.shape[2]
    picker = (
        segment_adapter_ids[:, None] == jnp.arange(adapters, dtype=jnp.int32)[None, :]
    ).astype(jnp.bfloat16)
    chosen = jnp.einsum(
        "sa,aqf->sqf", picker, slice_list, preferred_element_type=jnp.float32
    ).astype(jnp.bfloat16)
    own_ranks = lax.dynamic_slice_in_dim(down_proj, tp_index * rank_part, rank_part, 1)
    spread = (member.T.astype(jnp.bfloat16)[:, :, None] * own_ranks[:, None, :]).reshape(
        total_rows, seg_count * rank_part
    )
    delta_cols = lax.dot_general(
        chosen.reshape(seg_count * rank_part, ff_dev),
        spread,
        (((0,), (1,)), ((), ())),
        preferred_element_type=jnp.float32,
    )
    upper = tp_index >= tp_count // 2
    blank = jnp.zeros_like(delta_cols)
    policy_terms = base_terms + jnp.stack(
        [jnp.where(upper, blank, delta_cols), jnp.where(upper, delta_cols, blank)]
    )
    halves = lax.psum_scatter(
        jnp.stack([base_terms, policy_terms]), "tensor", scatter_dimension=3, tiled=True
    )
    ref_hidden = (jax.nn.silu(halves[0, 0]) * halves[0, 1]).astype(jnp.bfloat16)
    pol_hidden = (jax.nn.silu(halves[1, 0]) * halves[1, 1]).astype(jnp.bfloat16)
    ref_vals = 4.0 * jnp.tanh(ref_hidden.astype(jnp.float32) * 0.25)
    pol_vals = 4.0 * jnp.tanh(pol_hidden.astype(jnp.float32) * 0.25)
    pol_exp = jnp.exp(pol_vals)
    first_half = tp_index * rows_half

    def placed(values):
        return lax.dynamic_update_slice_in_dim(
            jnp.zeros((total_rows,), jnp.float32), values, first_half, 0
        )

    ref_sum, pol_sum, cross_sum = lax.psum(
        (
            placed(jnp.sum(jnp.exp(ref_vals), axis=0)),
            placed(jnp.sum(pol_exp, axis=0)),
            placed(jnp.sum(pol_exp * (pol_vals - ref_vals), axis=0)),
        ),
        ("dp", "tensor"),
    )
    kl_row = cross_sum / pol_sum - jnp.log(pol_sum) + jnp.log(ref_sum)
    seg_kl = jnp.sum(live_rows.astype(jnp.float32) * kl_row[None, :], axis=1) / counts
    return (ref_hidden, pol_hidden, seg_kl)


MESH = pl.DeviceIdType.MESH


def ring_place(dp_index, count):
    odd = dp_index % 2
    return odd * (count - 1 - dp_index // 2) + (1 - odd) * (dp_index // 2)


def ring_index(place, count):
    upper = place // (count // 2)
    return (1 - upper) * 2 * place + upper * (2 * (count - 1 - place) + 1)


def gather_project(
    dp_count, tp_count, group_count, unit_chunk,
    tokens, gate, up, down, adapter_up, owned,
    own_out, peer_out, adapters_out, down_out,
    tok_buf, weights, down_buf, parts, contrib, contrib_peer, published, heard,
    load_sem, ring_send, ring_recv, ad_send, ad_recv, pass_send, pass_recv,
    part_send, part_recv, con_send, con_recv, pub_send, pub_recv,
):
    half = dp_count // 2
    rows = tokens.shape[0]
    units = gate.shape[0]
    ranks = adapter_up.shape[0]
    me = lax.axis_index("dp")
    core = lax.axis_index("tensor")
    group = lax.axis_index("groups")
    place = ring_place(me, dp_count)
    right = ring_index((place + 1) % dp_count, dp_count)
    left = ring_index((place + dp_count - 1) % dp_count, dp_count)
    other_core = 1 - core
    other_group = 1 - group

    barrier = pltpu.get_barrier_semaphore()
    for k in range(1, dp_count):
        pl.semaphore_signal(barrier, inc=1, device_id={"dp": (me + k) % dp_count}, device_id_type=MESH)
    pl.semaphore_signal(barrier, inc=1, device_id={"tensor": other_core}, device_id_type=MESH)
    pl.semaphore_signal(barrier, inc=1, device_id={"groups": other_group}, device_id_type=MESH)
    pl.semaphore_wait(barrier, dp_count + 1)

    def block(slot):
        return tok_buf.at[pl.ds(slot * rows, rows)]

    def send(src, dst, sem, axis, target, sends, recvs):
        copy = pltpu.make_async_remote_copy(
            src_ref=src, dst_ref=dst, send_sem=sends.at[sem], recv_sem=recvs.at[sem],
            device_id={axis: target}, device_id_type=MESH,
        )
        copy.start()
        return copy

    last = dp_count - 1
    cut = rows // 2
    cw = send(tokens, block(1), 0, "dp", right, ring_send, ring_recv)
    ccw = send(tokens, block(2), 1, "dp", left, ring_send, ring_recv)

    loads = [
        pltpu.make_async_copy(tokens, block(0), load_sem.at[0]),
        pltpu.make_async_copy(gate, weights.at[0], load_sem.at[1]),
        pltpu.make_async_copy(up, weights.at[1], load_sem.at[2]),
        pltpu.make_async_copy(down, down_buf, load_sem.at[3]),
    ]
    for load in loads:
        load.start()

    share = ranks // group_count
    mine = pl.ds(pl.multiple_of(group * share, 16), share)
    landing = pl.ds(pl.multiple_of(core * ranks + group * share, 16), share)
    ad_copies = []
    for k in range(1, dp_count):
        target = (me + k) % dp_count
        ad_copies.append(send(
            adapter_up.at[mine, pl.ds(pl.multiple_of(target * units, 128), units)],
            adapters_out.at[me, landing], k, "dp", target, ad_send, ad_recv,
        ))
    ad_local = pltpu.make_async_copy(
        adapter_up.at[mine, pl.ds(pl.multiple_of(me * units, 128), units)],
        adapters_out.at[me, landing], load_sem.at[4],
    )
    ad_local.start()
    for load in loads:
        load.wait()

    def project(slot, blocks):
        def chunk(step, carry):
            which = step // (units // unit_chunk)
            first = pl.multiple_of((step % (units // unit_chunk)) * unit_chunk, unit_chunk)
            value = lax.dot_general(
                weights[which, pl.ds(first, unit_chunk), :],
                tok_buf[pl.ds(slot * rows, blocks * rows), :],
                (((1,), (1,)), ((), ())), preferred_element_type=jnp.float32,
            )
            for b in range(blocks):
                parts[slot + b, which, pl.ds(first, unit_chunk), :] = value[:, b * rows:(b + 1) * rows]
            return carry

        lax.fori_loop(0, 2 * (units // unit_chunk), chunk, 0)

    def project_down(slot, blocks):
        contrib[pl.ds(slot * rows, blocks * rows), :] = jnp.dot(
            tok_buf[pl.ds(slot * rows, blocks * rows), :], down_buf[...],
            preferred_element_type=jnp.float32,
        )
        for j in range(slot, slot + blocks):
            @pl.when(slot_block[j] // per_core != core)
            def _():
                contrib_copy(j).start()

    per_core = dp_count // tp_count
    slot_place = [place]
    for s in range(1, half):
        slot_place += [(place + dp_count - s) % dp_count, (place + s) % dp_count]
    slot_place.append((place + half) % dp_count)
    slot_block = [ring_index(q, dp_count) for q in slot_place]

    def part_copy(slot):
        where = slot_block[slot] % per_core
        return pltpu.make_async_remote_copy(
            src_ref=parts.at[slot], dst_ref=peer_out.at[where],
            send_sem=part_send.at[slot], recv_sem=part_recv.at[where],
            device_id={"tensor": other_core}, device_id_type=MESH,
        )

    def own_copy(slot):
        where = slot_block[slot] % per_core
        return pltpu.make_async_copy(parts.at[slot], own_out.at[where], part_send.at[slot])

    def contrib_copy(slot):
        where = slot_block[slot] % per_core
        return pltpu.make_async_remote_copy(
            src_ref=contrib.at[pl.ds(slot * rows, rows)], dst_ref=contrib_peer.at[where],
            send_sem=con_send.at[slot], recv_sem=con_recv.at[where],
            device_id={"tensor": other_core}, device_id_type=MESH,
        )

    def publish_copy(where, k):
        return pltpu.make_async_remote_copy(
            src_ref=published.at[where], dst_ref=heard.at[k - 1, where],
            send_sem=pub_send.at[k - 1, where], recv_sem=pub_recv.at[k - 1, where],
            device_id={"dp": (me + k) % dp_count}, device_id_type=MESH,
        )

    def publish(slot):
        where = slot_block[slot] % per_core

        @pl.when(slot_block[slot] // per_core == core)
        def _():
            contrib_copy(slot).wait_recv()
            total = contrib[pl.ds(slot * rows, rows), :] + contrib_peer[where]
            published[where] = (total * owned[slot_block[slot], 0:1, :]).astype(published.dtype)
            for k in range(1, dp_count):
                publish_copy(where, k).start()

    def hand_over(slot):
        @pl.when(slot_block[slot] // per_core == core)
        def _():
            own_copy(slot).start()

        @pl.when(slot_block[slot] // per_core != core)
        def _():
            part_copy(slot).start()

    project_down(0, 1)
    project(0, 1)
    hand_over(0)
    publish(0)
    sent = [cw, ccw]
    passes = []
    for s in range(1, half):
        cw.wait_recv()
        ccw.wait_recv()
        if s < half - 1:
            cw = send(block(2 * s - 1), block(2 * s + 1), 2 * s, "dp", right, ring_send, ring_recv)
            ccw = send(block(2 * s), block(2 * s + 2), 2 * s + 1, "dp", left, ring_send, ring_recv)
        else:
            a, b = (2 * s - 1) * rows, 2 * s * rows + cut
            z = last * rows
            cw = send(tok_buf.at[pl.ds(a, cut)], tok_buf.at[pl.ds(z, cut)],
                      2 * s, "dp", right, ring_send, ring_recv)
            ccw = send(tok_buf.at[pl.ds(b, cut)], tok_buf.at[pl.ds(z + cut, cut)],
                       2 * s + 1, "dp", left, ring_send, ring_recv)
        sent += [cw, ccw]
        project_down(2 * s - 1, 2)
        project(2 * s - 1, 2)
        hand_over(2 * s - 1)
        hand_over(2 * s)
        publish(2 * s - 1)
        publish(2 * s)
        if s == half - 2:
            for copy in ad_copies:
                copy.wait_recv()
            ad_local.wait()
            region = adapters_out.at[:, landing]
            passes.append(send(region, region, 0, "groups", other_group, pass_send, pass_recv))
        if s == half - 1:
            passes[0].wait_recv()
            region = adapters_out.at[:, pl.ds(pl.multiple_of(core * ranks, 16), ranks)]
            passes.append(send(region, region, 1, "tensor", other_core, pass_send, pass_recv))
    cw.wait_recv()
    ccw.wait_recv()
    project_down(last, 1)
    publish(last)
    project(last, 1)
    hand_over(last)
    for where in range(per_core):
        for k in range(1, dp_count):
            publish_copy(where, k).wait_recv()
        total = published[where].astype(jnp.float32)
        for k in range(1, dp_count):
            total = total + heard[k - 1, where].astype(jnp.float32)
        down_out[pl.ds(where * rows, rows), :] = total.astype(down_out.dtype)

    for copy in sent + ad_copies + passes:
        copy.wait_send()
    passes[1].wait_recv()
    for slot in range(dp_count):
        @pl.when(slot_block[slot] // per_core == core)
        def _():
            own_copy(slot).wait()

        @pl.when(slot_block[slot] // per_core != core)
        def _():
            part_copy(slot).wait_send()
            contrib_copy(slot).wait_send()

    for where in range(per_core):
        for k in range(1, dp_count):
            publish_copy(where, k).wait_send()
        pltpu.make_async_remote_copy(
            src_ref=parts.at[where], dst_ref=peer_out.at[where],
            send_sem=part_send.at[where], recv_sem=part_recv.at[where],
            device_id={"tensor": other_core}, device_id_type=MESH,
        ).wait_recv()


def finish(ids, own, peer, adapters, down_proj, ref_out, pol_out, sums):
    blocks = own.shape[0]
    rows = own.shape[3]
    ranks = down_proj.shape[1] // 2

    @pl.when(pl.program_id(0) == 0)
    def _():
        sums[...] = jnp.zeros_like(sums)

    def silu(v):
        return v / (1.0 + jnp.exp(-v))

    contract = (((0,), (1,)), ((), ()))
    for j in range(blocks):
        columns = slice(j * rows, (j + 1) * rows)
        gate = own[j, 0] + peer[j, 0]
        up = own[j, 1] + peer[j, 1]
        chosen = adapters[ids[j]]
        ref_hidden = (silu(gate) * up).astype(jnp.bfloat16)
        ref_out[:, columns] = ref_hidden
        gate = gate + lax.dot_general(
            chosen[:ranks], down_proj[columns, :ranks], contract, preferred_element_type=jnp.float32
        )
        up = up + lax.dot_general(
            chosen[ranks:], down_proj[columns, ranks:], contract, preferred_element_type=jnp.float32
        )
        pol_hidden = (silu(gate) * up).astype(jnp.bfloat16)
        pol_out[:, columns] = pol_hidden
        ref_vals = 4.0 * jnp.tanh(ref_hidden.astype(jnp.float32) * 0.25)
        pol_vals = 4.0 * jnp.tanh(pol_hidden.astype(jnp.float32) * 0.25)
        pol_exp = jnp.exp(pol_vals)
        for k, value in enumerate((jnp.exp(ref_vals), pol_exp, pol_exp * (pol_vals - ref_vals))):
            sums[k, :, columns] += value.reshape(-1, 8, rows).sum(axis=0)


def divergence(dp_count, sums, live, out, mine, heard, halves, send_sem, recv_sem):
    me = lax.axis_index("dp")
    other_core = 1 - lax.axis_index("tensor")
    barrier = pltpu.get_barrier_semaphore()
    for k in range(1, dp_count):
        pl.semaphore_signal(barrier, inc=1, device_id={"dp": (me + k) % dp_count}, device_id_type=MESH)
    pl.semaphore_signal(barrier, inc=1, device_id={"tensor": other_core}, device_id_type=MESH)
    for k in range(3):
        mine[k:k + 1, :] = jnp.sum(sums[k], axis=0, keepdims=True)
    mine[3:8, :] = jnp.zeros((5, mine.shape[1]), jnp.float32)
    pl.semaphore_wait(barrier, dp_count)
    copies = []
    for k in range(1, dp_count):
        copies.append(pltpu.make_async_remote_copy(
            src_ref=mine, dst_ref=heard.at[me], send_sem=send_sem.at[k], recv_sem=recv_sem.at[k],
            device_id={"dp": (me + k) % dp_count}, device_id_type=MESH,
        ))
        copies[-1].start()
    for copy in copies:
        copy.wait_recv()
    heard[me] = mine[...]
    total = heard[0]
    for k in range(1, dp_count):
        total = total + heard[k]
    ref_sum, pol_sum, cross_sum = total[0:1], total[1:2], total[2:3]
    kl_row = cross_sum / pol_sum - jnp.log(pol_sum) + jnp.log(ref_sum)
    part = jnp.sum(live[...] * kl_row, axis=1, keepdims=True)
    halves[0] = jnp.broadcast_to(part, (8, 128))
    swap = pltpu.make_async_remote_copy(
        src_ref=halves.at[0], dst_ref=halves.at[1], send_sem=send_sem.at[0], recv_sem=recv_sem.at[0],
        device_id={"tensor": other_core}, device_id_type=MESH,
    )
    swap.start()
    swap.wait()
    for copy in copies:
        copy.wait_send()
    out[...] = halves[0] + halves[1]


def kernel_shards(
    tokens, gate_weight_base, up_weight_base, adapter_down_stack, adapter_up_stack,
    segment_block_counts, segment_adapter_ids, segment_live_rows,
):
    dp_count = lax.axis_size("dp")
    tp_count = lax.axis_size("tensor")
    group_count = lax.axis_size("groups")
    dp_index = lax.axis_index("dp")
    tp_index = lax.axis_index("tensor")
    local_rows, features = tokens.shape
    units = gate_weight_base.shape[0]
    ranks = adapter_up_stack.shape[1]
    total_rows = local_rows * dp_count
    per_core = dp_count // tp_count
    rows_half = total_rows // tp_count
    member, live_rows, counts = segment_tables(segment_block_counts, segment_live_rows, total_rows)
    row_adapter = jnp.sum(member.astype(jnp.int32) * segment_adapter_ids[:, None], axis=0)
    f32, bf16 = jnp.float32, jnp.bfloat16
    any_spec = pl.BlockSpec(memory_space=pl.ANY)
    dma = pltpu.SemaphoreType.DMA
    owned = jnp.broadcast_to(
        (row_adapter[::local_rows] == dp_index).astype(f32)[:, None, None],
        (dp_count, 8, tp_count * ranks),
    )
    vmem_spec = pl.BlockSpec(memory_space=pltpu.VMEM)
    own, peer, adapters, own_down = pl.pallas_call(
        functools.partial(gather_project, dp_count, tp_count, group_count, units // 2),
        out_shape=(
            jax.ShapeDtypeStruct((per_core, 2, units, local_rows), f32),
            jax.ShapeDtypeStruct((per_core, 2, units, local_rows), f32),
            jax.ShapeDtypeStruct((dp_count, tp_count * ranks, units), bf16),
            jax.ShapeDtypeStruct((rows_half, tp_count * ranks), bf16),
        ),
        in_specs=[any_spec] * 5 + [vmem_spec],
        out_specs=(any_spec,) * 3 + (vmem_spec,),
        scratch_shapes=[
            pltpu.VMEM((total_rows, features), bf16),
            pltpu.VMEM((2, units, features), bf16),
            pltpu.VMEM((features, tp_count * ranks), bf16),
            pltpu.VMEM((dp_count, 2, units, local_rows), f32),
            pltpu.VMEM((total_rows, tp_count * ranks), f32),
            pltpu.VMEM((per_core, local_rows, tp_count * ranks), f32),
            pltpu.VMEM((per_core, local_rows, tp_count * ranks), bf16),
            pltpu.VMEM((dp_count - 1, per_core, local_rows, tp_count * ranks), bf16),
            dma((5,)), dma((dp_count,)), dma((dp_count,)), dma((dp_count,)), dma((dp_count,)),
            dma((2,)), dma((2,)), dma((dp_count,)), dma((per_core,)), dma((dp_count,)), dma((per_core,)),
            dma((dp_count - 1, per_core)), dma((dp_count - 1, per_core)),
        ],
        compiler_params=pltpu.CompilerParams(
            collective_id=0, has_side_effects=True, vmem_limit_bytes=60 * 1024 * 1024
        ),
        name="gather_project",
    )(tokens, gate_weight_base, up_weight_base, adapter_down_stack[0], adapter_up_stack[0], owned)
    own_ids = lax.dynamic_slice_in_dim(row_adapter[::local_rows], tp_index * per_core, per_core, 0)
    chunk = 256
    ref_hidden, pol_hidden, sums = pl.pallas_call(
        finish,
        out_shape=(
            jax.ShapeDtypeStruct((units, rows_half), bf16),
            jax.ShapeDtypeStruct((units, rows_half), bf16),
            jax.ShapeDtypeStruct((3, 8, rows_half), f32),
        ),
        grid_spec=pltpu.PrefetchScalarGridSpec(
            num_scalar_prefetch=1,
            grid=(units // chunk,),
            in_specs=[
                pl.BlockSpec((per_core, 2, chunk, local_rows), lambda u, ids: (0, 0, u, 0)),
                pl.BlockSpec((per_core, 2, chunk, local_rows), lambda u, ids: (0, 0, u, 0)),
                pl.BlockSpec((dp_count, tp_count * ranks, chunk), lambda u, ids: (0, 0, u)),
                pl.BlockSpec((rows_half, tp_count * ranks), lambda u, ids: (0, 0)),
            ],
            out_specs=[
                pl.BlockSpec((chunk, rows_half), lambda u, ids: (u, 0)),
                pl.BlockSpec((chunk, rows_half), lambda u, ids: (u, 0)),
                pl.BlockSpec((3, 8, rows_half), lambda u, ids: (0, 0, 0)),
            ],
        ),
        compiler_params=pltpu.CompilerParams(vmem_limit_bytes=60 * 1024 * 1024),
        name="finish",
    )(own_ids, own, peer, adapters, own_down)
    seg_count = live_rows.shape[0]
    spread = jnp.zeros((8, total_rows), f32).at[:seg_count].set(live_rows.astype(f32))
    own_live = lax.dynamic_slice_in_dim(spread, tp_index * rows_half, rows_half, 1)
    seg_sums = pl.pallas_call(
        functools.partial(divergence, dp_count),
        out_shape=jax.ShapeDtypeStruct((8, 128), f32),
        in_specs=[vmem_spec] * 2,
        out_specs=vmem_spec,
        scratch_shapes=[
            pltpu.VMEM((8, rows_half), f32),
            pltpu.VMEM((dp_count, 8, rows_half), f32),
            pltpu.VMEM((2, 8, 128), f32),
            dma((dp_count,)), dma((dp_count,)),
        ],
        compiler_params=pltpu.CompilerParams(collective_id=1, has_side_effects=True),
        name="divergence",
    )(sums, own_live)
    seg_kl = seg_sums[:seg_count, 0] / counts
    return (ref_hidden, pol_hidden, seg_kl)


def pick_shards(*args):
    rows = args[0].shape[0]
    units = args[1].shape[0]
    sizes = (lax.axis_size("groups"), lax.axis_size("tensor"))
    fits = rows == BLOCK and units % 256 == 0 and sizes == (2, 2) and lax.axis_size("dp") % 4 == 0
    return kernel_shards(*args) if fits else shards(*args)


def solution(mesh):
    in_specs = (
        P(("groups", "dp"), "tensor"),
        P("dp", "tensor"),
        P("dp", "tensor"),
        P("dp", "tensor", None),
        P("dp", "tensor", None),
        P("groups"),
        P("groups"),
        P("groups"),
    )
    out_specs = (P("dp", ("groups", "tensor")), P("dp", ("groups", "tensor")), P("groups"))
    return jax.shard_map(pick_shards, mesh=mesh, in_specs=in_specs, out_specs=out_specs, check_vma=False)
```

```python
import functools
import jax
import jax.numpy as jnp
from jax import lax
from jax.experimental import pallas as pl
from jax.experimental.pallas import tpu as pltpu
from jax.sharding import PartitionSpec as P

BLOCK = 128


def spread_2(value, axis, root):
    mine = lax.axis_index(axis) == root
    return lax.psum(jnp.where(mine, value, jnp.zeros_like(value)), axis)


def segment_tables(segment_block_counts, segment_live_rows, total_rows):
    order = jnp.arange(segment_block_counts.shape[0])
    before = order[None, :] <= order[:, None]
    seg_ends = jnp.sum(jnp.where(before, segment_block_counts[None, :], 0), axis=1)
    starts = seg_ends - segment_block_counts
    row_ids = jnp.arange(total_rows, dtype=jnp.int32)
    blocks = row_ids // BLOCK
    member = (blocks[None, :] >= starts[:, None]) & (blocks[None, :] < seg_ends[:, None])
    live_limit = (seg_ends - 1) * BLOCK + segment_live_rows
    live_rows = member & (row_ids[None, :] < live_limit[:, None])
    counts = (live_limit - starts * BLOCK).astype(jnp.float32)
    return (member, live_rows, counts)


def project_tokens(tokens, gate_weight_base, up_weight_base, adapter_down_matrix, owned_rows):
    contract = (((1,), (1,)), ((), ()))
    rank_pair = adapter_down_matrix.shape[1]
    block_rows = lax.all_gather(tokens, "dp", axis=0, tiled=True)
    row_count = block_rows.shape[0]
    gate_part = lax.dot_general(
        gate_weight_base, block_rows, contract, preferred_element_type=jnp.float32
    )
    up_part = lax.dot_general(
        up_weight_base, block_rows, contract, preferred_element_type=jnp.float32
    )
    base_terms = jnp.stack([gate_part, up_part])
    contrib = lax.cond(
        jnp.any(owned_rows),
        lambda: jnp.dot(block_rows, adapter_down_matrix, preferred_element_type=jnp.float32)
        * owned_rows[:, None].astype(jnp.float32),
        lambda: jnp.zeros((row_count, rank_pair), jnp.float32),
    )
    return (base_terms, contrib)


def shards(
    tokens,
    gate_weight_base,
    up_weight_base,
    adapter_down_stack,
    adapter_up_stack,
    segment_block_counts,
    segment_adapter_ids,
    segment_live_rows,
):
    dp_count = lax.axis_size("dp")
    tp_count = lax.axis_size("tensor")
    dp_index = lax.axis_index("dp")
    tp_index = lax.axis_index("tensor")
    local_rows = tokens.shape[0]
    total_rows = local_rows * dp_count
    rows_half = total_rows // tp_count
    seg_count = segment_block_counts.shape[0]
    member, live_rows, counts = segment_tables(segment_block_counts, segment_live_rows, total_rows)
    adapter_down_matrix = adapter_down_stack[0]
    rank_pair = adapter_down_matrix.shape[1]
    base_terms, unused_terms = project_tokens(
        tokens,
        gate_weight_base,
        up_weight_base,
        adapter_down_matrix,
        jnp.zeros((total_rows,), jnp.bool_),
    )
    home_first = dp_index * local_rows
    home_member = lax.dynamic_slice_in_dim(member, home_first, local_rows, 1).astype(jnp.float32)

    def fetch_slot(buffer_slot, accum):
        fetched = spread_2(adapter_down_matrix, "dp", segment_adapter_ids[buffer_slot])
        return (
            accum
            + jnp.dot(tokens, fetched, preferred_element_type=jnp.float32)
            * home_member[buffer_slot][:, None]
        )

    home_terms = lax.fori_loop(
        0, seg_count, fetch_slot, jnp.zeros((local_rows, rank_pair), jnp.float32)
    )
    down_terms = lax.dynamic_update_slice_in_dim(
        jnp.zeros((total_rows, rank_pair), jnp.float32), home_terms, home_first, 0
    )
    down_proj = lax.psum(down_terms, ("dp", "tensor")).astype(jnp.bfloat16)
    slice_list = lax.all_to_all(adapter_up_stack, "dp", split_axis=2, concat_axis=0, tiled=True)
    adapters = slice_list.shape[0]
    rank_part = slice_list.shape[1]
    ff_dev = slice_list.shape[2]
    picker = (
        segment_adapter_ids[:, None] == jnp.arange(adapters, dtype=jnp.int32)[None, :]
    ).astype(jnp.bfloat16)
    chosen = jnp.einsum(
        "sa,aqf->sqf", picker, slice_list, preferred_element_type=jnp.float32
    ).astype(jnp.bfloat16)
    own_ranks = lax.dynamic_slice_in_dim(down_proj, tp_index * rank_part, rank_part, 1)
    spread = (member.T.astype(jnp.bfloat16)[:, :, None] * own_ranks[:, None, :]).reshape(
        total_rows, seg_count * rank_part
    )
    delta_cols = lax.dot_general(
        chosen.reshape(seg_count * rank_part, ff_dev),
        spread,
        (((0,), (1,)), ((), ())),
        preferred_element_type=jnp.float32,
    )
    upper = tp_index >= tp_count // 2
    blank = jnp.zeros_like(delta_cols)
    policy_terms = base_terms + jnp.stack(
        [jnp.where(upper, blank, delta_cols), jnp.where(upper, delta_cols, blank)]
    )
    halves = lax.psum_scatter(
        jnp.stack([base_terms, policy_terms]), "tensor", scatter_dimension=3, tiled=True
    )
    ref_hidden = (jax.nn.silu(halves[0, 0]) * halves[0, 1]).astype(jnp.bfloat16)
    pol_hidden = (jax.nn.silu(halves[1, 0]) * halves[1, 1]).astype(jnp.bfloat16)
    ref_vals = 4.0 * jnp.tanh(ref_hidden.astype(jnp.float32) * 0.25)
    pol_vals = 4.0 * jnp.tanh(pol_hidden.astype(jnp.float32) * 0.25)
    pol_exp = jnp.exp(pol_vals)
    first_half = tp_index * rows_half

    def placed(values):
        return lax.dynamic_update_slice_in_dim(
            jnp.zeros((total_rows,), jnp.float32), values, first_half, 0
        )

    ref_sum, pol_sum, cross_sum = lax.psum(
        (
            placed(jnp.sum(jnp.exp(ref_vals), axis=0)),
            placed(jnp.sum(pol_exp, axis=0)),
            placed(jnp.sum(pol_exp * (pol_vals - ref_vals), axis=0)),
        ),
        ("dp", "tensor"),
    )
    kl_row = cross_sum / pol_sum - jnp.log(pol_sum) + jnp.log(ref_sum)
    seg_kl = jnp.sum(live_rows.astype(jnp.float32) * kl_row[None, :], axis=1) / counts
    return (ref_hidden, pol_hidden, seg_kl)


MESH = pl.DeviceIdType.MESH


def ring_place(dp_index, count):
    odd = dp_index % 2
    return odd * (count - 1 - dp_index // 2) + (1 - odd) * (dp_index // 2)


def ring_index(place, count):
    upper = place // (count // 2)
    return (1 - upper) * 2 * place + upper * (2 * (count - 1 - place) + 1)


def gather_project(
    dp_count, tp_count, group_count, unit_chunk,
    tokens, gate, up, down, adapter_up, owned,
    own_out, peer_out, adapters_out, down_out,
    tok_buf, weights, down_buf, parts, contrib, contrib_peer, published, heard, reduced, gathered,
    load_sem, ring_send, ring_recv, ad_send, ad_recv, pass_send, pass_recv,
    part_send, part_recv, con_send, con_recv, pub_send, pub_recv,
    red_send, red_recv,
):
    half = dp_count // 2
    rows = tokens.shape[0]
    units = gate.shape[0]
    ranks = adapter_up.shape[0]
    me = lax.axis_index("dp")
    core = lax.axis_index("tensor")
    group = lax.axis_index("groups")
    place = ring_place(me, dp_count)
    right = ring_index((place + 1) % dp_count, dp_count)
    left = ring_index((place + dp_count - 1) % dp_count, dp_count)
    other_core = 1 - core
    other_group = 1 - group

    barrier = pltpu.get_barrier_semaphore()
    for k in range(1, dp_count):
        pl.semaphore_signal(barrier, inc=1, device_id={"dp": (me + k) % dp_count}, device_id_type=MESH)
    pl.semaphore_signal(barrier, inc=1, device_id={"tensor": other_core}, device_id_type=MESH)
    pl.semaphore_signal(barrier, inc=1, device_id={"groups": other_group}, device_id_type=MESH)
    pl.semaphore_wait(barrier, dp_count + 1)

    def block(slot):
        return tok_buf.at[pl.ds(slot * rows, rows)]

    def send(src, dst, sem, axis, target, sends, recvs):
        copy = pltpu.make_async_remote_copy(
            src_ref=src, dst_ref=dst, send_sem=sends.at[sem], recv_sem=recvs.at[sem],
            device_id={axis: target}, device_id_type=MESH,
        )
        copy.start()
        return copy

    last = dp_count - 1
    cut = rows // 2
    cw = send(tokens, block(1), 0, "dp", right, ring_send, ring_recv)
    ccw = send(tokens, block(2), 1, "dp", left, ring_send, ring_recv)

    loads = [
        pltpu.make_async_copy(tokens, block(0), load_sem.at[0]),
        pltpu.make_async_copy(gate, weights.at[0], load_sem.at[1]),
        pltpu.make_async_copy(up, weights.at[1], load_sem.at[2]),
        pltpu.make_async_copy(down, down_buf, load_sem.at[3]),
    ]
    for load in loads:
        load.start()

    share = ranks // group_count
    mine = pl.ds(pl.multiple_of(group * share, 16), share)
    landing = pl.ds(pl.multiple_of(core * ranks + group * share, 16), share)
    ad_copies = []
    for k in range(1, dp_count):
        target = (me + k) % dp_count
        ad_copies.append(send(
            adapter_up.at[mine, pl.ds(pl.multiple_of(target * units, 128), units)],
            adapters_out.at[me, landing], k, "dp", target, ad_send, ad_recv,
        ))
    ad_local = pltpu.make_async_copy(
        adapter_up.at[mine, pl.ds(pl.multiple_of(me * units, 128), units)],
        adapters_out.at[me, landing], load_sem.at[4],
    )
    ad_local.start()
    for load in loads:
        load.wait()

    def project(slot, blocks, matrices=(0, 2)):
        def chunk(step, carry):
            which = step // (units // unit_chunk)
            first = pl.multiple_of((step % (units // unit_chunk)) * unit_chunk, unit_chunk)
            value = lax.dot_general(
                weights[which, pl.ds(first, unit_chunk), :],
                tok_buf[pl.ds(slot * rows, blocks * rows), :],
                (((1,), (1,)), ((), ())), preferred_element_type=jnp.float32,
            )
            for b in range(blocks):
                parts[slot + b, which, pl.ds(first, unit_chunk), :] = value[:, b * rows:(b + 1) * rows]
            return carry

        per_matrix = units // unit_chunk
        lax.fori_loop(matrices[0] * per_matrix, matrices[1] * per_matrix, chunk, 0)

    def project_down(slot, blocks):
        contrib[pl.ds(slot * rows, blocks * rows), :] = jnp.dot(
            tok_buf[pl.ds(slot * rows, blocks * rows), :], down_buf[...],
            preferred_element_type=jnp.float32,
        )
        for j in range(slot, slot + blocks):
            @pl.when(slot_block[j] // per_core != core)
            def _():
                contrib_copy(j).start()

    per_core = dp_count // tp_count
    slot_place = [place]
    for s in range(1, half):
        slot_place += [(place + dp_count - s) % dp_count, (place + s) % dp_count]
    slot_place.append((place + half) % dp_count)
    slot_block = [ring_index(q, dp_count) for q in slot_place]

    def part_copy(slot):
        where = slot_block[slot] % per_core
        return pltpu.make_async_remote_copy(
            src_ref=parts.at[slot], dst_ref=peer_out.at[where],
            send_sem=part_send.at[slot], recv_sem=part_recv.at[where],
            device_id={"tensor": other_core}, device_id_type=MESH,
        )

    def own_copy(slot):
        where = slot_block[slot] % per_core
        return pltpu.make_async_copy(parts.at[slot], own_out.at[where], part_send.at[slot])

    def contrib_copy(slot):
        where = slot_block[slot] % per_core
        return pltpu.make_async_remote_copy(
            src_ref=contrib.at[pl.ds(slot * rows, rows)], dst_ref=contrib_peer.at[where],
            send_sem=con_send.at[slot], recv_sem=con_recv.at[where],
            device_id={"tensor": other_core}, device_id_type=MESH,
        )

    strip = rows // dp_count

    def publish_copy(where, k):
        target = (me + k) % dp_count
        return pltpu.make_async_remote_copy(
            src_ref=published.at[where, pl.ds(pl.multiple_of(target * strip, 16), strip)],
            dst_ref=heard.at[k - 1, where],
            send_sem=pub_send.at[k - 1, where], recv_sem=pub_recv.at[k - 1, where],
            device_id={"dp": (me + k) % dp_count}, device_id_type=MESH,
        )

    def publish(slot):
        where = slot_block[slot] % per_core

        @pl.when(slot_block[slot] // per_core == core)
        def _():
            contrib_copy(slot).wait_recv()
            total = contrib[pl.ds(slot * rows, rows), :] + contrib_peer[where]
            published[where] = (total * owned[slot_block[slot], 0:1, :]).astype(published.dtype)
            for k in range(1, dp_count):
                publish_copy(where, k).start()

    def hand_over(slot):
        @pl.when(slot_block[slot] // per_core == core)
        def _():
            own_copy(slot).start()

        @pl.when(slot_block[slot] // per_core != core)
        def _():
            part_copy(slot).start()

    project_down(0, 1)
    project(0, 1)
    hand_over(0)
    publish(0)
    sent = [cw, ccw]
    passes = []
    for s in range(1, half):
        cw.wait_recv()
        ccw.wait_recv()
        if s < half - 1:
            cw = send(block(2 * s - 1), block(2 * s + 1), 2 * s, "dp", right, ring_send, ring_recv)
            ccw = send(block(2 * s), block(2 * s + 2), 2 * s + 1, "dp", left, ring_send, ring_recv)
        else:
            a, b = (2 * s - 1) * rows, 2 * s * rows + cut
            z = last * rows
            cw = send(tok_buf.at[pl.ds(a, cut)], tok_buf.at[pl.ds(z, cut)],
                      2 * s, "dp", right, ring_send, ring_recv)
            ccw = send(tok_buf.at[pl.ds(b, cut)], tok_buf.at[pl.ds(z + cut, cut)],
                       2 * s + 1, "dp", left, ring_send, ring_recv)
        sent += [cw, ccw]
        project_down(2 * s - 1, 2)
        project(2 * s - 1, 2)
        hand_over(2 * s - 1)
        hand_over(2 * s)
        publish(2 * s - 1)
        publish(2 * s)
        if s == half - 2:
            for copy in ad_copies:
                copy.wait_recv()
            ad_local.wait()
            region = adapters_out.at[:, landing]
            passes.append(send(region, region, 0, "groups", other_group, pass_send, pass_recv))
        if s == half - 1:
            passes[0].wait_recv()
            region = adapters_out.at[:, pl.ds(pl.multiple_of(core * ranks, 16), ranks)]
            passes.append(send(region, region, 1, "tensor", other_core, pass_send, pass_recv))
    cw.wait_recv()
    ccw.wait_recv()
    project_down(last, 1)
    publish(last)
    project(last, 1, (0, 1))
    for where in range(per_core):
        for k in range(1, dp_count):
            publish_copy(where, k).wait_recv()
        total = published[where, pl.ds(pl.multiple_of(me * strip, 16), strip), :].astype(jnp.float32)
        for k in range(1, dp_count):
            total = total + heard[k - 1, where].astype(jnp.float32)
        reduced[where] = total.astype(reduced.dtype)
    spreads = []
    for k in range(1, dp_count):
        spreads.append(send(
            reduced, gathered.at[me], k, "dp", (me + k) % dp_count, red_send, red_recv
        ))
    project(last, 1, (1, 2))
    hand_over(last)
    for copy in spreads:
        copy.wait_recv()
    gathered[me] = reduced[...]
    for where in range(per_core):
        for d in range(dp_count):
            down_out[pl.ds(where * rows + d * strip, strip), :] = gathered[d, where]

    for copy in sent + ad_copies + passes + spreads:
        copy.wait_send()
    passes[1].wait_recv()
    for slot in range(dp_count):
        @pl.when(slot_block[slot] // per_core == core)
        def _():
            own_copy(slot).wait()

        @pl.when(slot_block[slot] // per_core != core)
        def _():
            part_copy(slot).wait_send()
            contrib_copy(slot).wait_send()

    for where in range(per_core):
        for k in range(1, dp_count):
            publish_copy(where, k).wait_send()
        pltpu.make_async_remote_copy(
            src_ref=parts.at[where], dst_ref=peer_out.at[where],
            send_sem=part_send.at[where], recv_sem=part_recv.at[where],
            device_id={"tensor": other_core}, device_id_type=MESH,
        ).wait_recv()


def finish(ids, own, peer, adapters, down_proj, ref_out, pol_out, sums):
    blocks = own.shape[0]
    rows = own.shape[3]
    ranks = down_proj.shape[1] // 2

    @pl.when(pl.program_id(0) == 0)
    def _():
        sums[...] = jnp.zeros_like(sums)

    def silu(v):
        return v / (1.0 + jnp.exp(-v))

    contract = (((0,), (1,)), ((), ()))
    for j in range(blocks):
        columns = slice(j * rows, (j + 1) * rows)
        gate = own[j, 0] + peer[j, 0]
        up = own[j, 1] + peer[j, 1]
        chosen = adapters[ids[j]]
        ref_hidden = (silu(gate) * up).astype(jnp.bfloat16)
        ref_out[:, columns] = ref_hidden
        gate = gate + lax.dot_general(
            chosen[:ranks], down_proj[columns, :ranks], contract, preferred_element_type=jnp.float32
        )
        up = up + lax.dot_general(
            chosen[ranks:], down_proj[columns, ranks:], contract, preferred_element_type=jnp.float32
        )
        pol_hidden = (silu(gate) * up).astype(jnp.bfloat16)
        pol_out[:, columns] = pol_hidden
        ref_vals = 4.0 * jnp.tanh(ref_hidden.astype(jnp.float32) * 0.25)
        pol_vals = 4.0 * jnp.tanh(pol_hidden.astype(jnp.float32) * 0.25)
        pol_exp = jnp.exp(pol_vals)
        for k, value in enumerate((jnp.exp(ref_vals), pol_exp, pol_exp * (pol_vals - ref_vals))):
            sums[k, :, columns] += value.reshape(-1, 8, rows).sum(axis=0)


def divergence(dp_count, sums, live, out, mine, heard, halves, send_sem, recv_sem):
    me = lax.axis_index("dp")
    other_core = 1 - lax.axis_index("tensor")
    barrier = pltpu.get_barrier_semaphore()
    for k in range(1, dp_count):
        pl.semaphore_signal(barrier, inc=1, device_id={"dp": (me + k) % dp_count}, device_id_type=MESH)
    pl.semaphore_signal(barrier, inc=1, device_id={"tensor": other_core}, device_id_type=MESH)
    for k in range(3):
        mine[k:k + 1, :] = jnp.sum(sums[k], axis=0, keepdims=True)
    mine[3:8, :] = jnp.zeros((5, mine.shape[1]), jnp.float32)
    pl.semaphore_wait(barrier, dp_count)
    copies = []
    for k in range(1, dp_count):
        copies.append(pltpu.make_async_remote_copy(
            src_ref=mine, dst_ref=heard.at[me], send_sem=send_sem.at[k], recv_sem=recv_sem.at[k],
            device_id={"dp": (me + k) % dp_count}, device_id_type=MESH,
        ))
        copies[-1].start()
    for copy in copies:
        copy.wait_recv()
    heard[me] = mine[...]
    total = heard[0]
    for k in range(1, dp_count):
        total = total + heard[k]
    ref_sum, pol_sum, cross_sum = total[0:1], total[1:2], total[2:3]
    kl_row = cross_sum / pol_sum - jnp.log(pol_sum) + jnp.log(ref_sum)
    part = jnp.sum(live[...] * kl_row, axis=1, keepdims=True)
    halves[0] = jnp.broadcast_to(part, (8, 128))
    swap = pltpu.make_async_remote_copy(
        src_ref=halves.at[0], dst_ref=halves.at[1], send_sem=send_sem.at[0], recv_sem=recv_sem.at[0],
        device_id={"tensor": other_core}, device_id_type=MESH,
    )
    swap.start()
    swap.wait()
    for copy in copies:
        copy.wait_send()
    out[...] = halves[0] + halves[1]


def kernel_shards(
    tokens, gate_weight_base, up_weight_base, adapter_down_stack, adapter_up_stack,
    segment_block_counts, segment_adapter_ids, segment_live_rows,
):
    dp_count = lax.axis_size("dp")
    tp_count = lax.axis_size("tensor")
    group_count = lax.axis_size("groups")
    dp_index = lax.axis_index("dp")
    tp_index = lax.axis_index("tensor")
    local_rows, features = tokens.shape
    units = gate_weight_base.shape[0]
    ranks = adapter_up_stack.shape[1]
    total_rows = local_rows * dp_count
    per_core = dp_count // tp_count
    rows_half = total_rows // tp_count
    member, live_rows, counts = segment_tables(segment_block_counts, segment_live_rows, total_rows)
    row_adapter = jnp.sum(member.astype(jnp.int32) * segment_adapter_ids[:, None], axis=0)
    f32, bf16 = jnp.float32, jnp.bfloat16
    any_spec = pl.BlockSpec(memory_space=pl.ANY)
    dma = pltpu.SemaphoreType.DMA
    owned = jnp.broadcast_to(
        (row_adapter[::local_rows] == dp_index).astype(f32)[:, None, None],
        (dp_count, 8, tp_count * ranks),
    )
    vmem_spec = pl.BlockSpec(memory_space=pltpu.VMEM)
    own, peer, adapters, own_down = pl.pallas_call(
        functools.partial(gather_project, dp_count, tp_count, group_count, units // 2),
        out_shape=(
            jax.ShapeDtypeStruct((per_core, 2, units, local_rows), f32),
            jax.ShapeDtypeStruct((per_core, 2, units, local_rows), f32),
            jax.ShapeDtypeStruct((dp_count, tp_count * ranks, units), bf16),
            jax.ShapeDtypeStruct((rows_half, tp_count * ranks), bf16),
        ),
        in_specs=[any_spec] * 5 + [vmem_spec],
        out_specs=(any_spec,) * 3 + (vmem_spec,),
        scratch_shapes=[
            pltpu.VMEM((total_rows, features), bf16),
            pltpu.VMEM((2, units, features), bf16),
            pltpu.VMEM((features, tp_count * ranks), bf16),
            pltpu.VMEM((dp_count, 2, units, local_rows), f32),
            pltpu.VMEM((total_rows, tp_count * ranks), f32),
            pltpu.VMEM((per_core, local_rows, tp_count * ranks), f32),
            pltpu.VMEM((per_core, local_rows, tp_count * ranks), bf16),
            pltpu.VMEM((dp_count - 1, per_core, local_rows // dp_count, tp_count * ranks), bf16),
            pltpu.VMEM((per_core, local_rows // dp_count, tp_count * ranks), bf16),
            pltpu.VMEM((dp_count, per_core, local_rows // dp_count, tp_count * ranks), bf16),
            dma((5,)), dma((dp_count,)), dma((dp_count,)), dma((dp_count,)), dma((dp_count,)),
            dma((2,)), dma((2,)), dma((dp_count,)), dma((per_core,)), dma((dp_count,)), dma((per_core,)),
            dma((dp_count - 1, per_core)), dma((dp_count - 1, per_core)), dma((dp_count,)), dma((dp_count,)),
        ],
        compiler_params=pltpu.CompilerParams(
            collective_id=0, has_side_effects=True, vmem_limit_bytes=60 * 1024 * 1024
        ),
        name="gather_project",
    )(tokens, gate_weight_base, up_weight_base, adapter_down_stack[0], adapter_up_stack[0], owned)
    own_ids = lax.dynamic_slice_in_dim(row_adapter[::local_rows], tp_index * per_core, per_core, 0)
    chunk = 256
    ref_hidden, pol_hidden, sums = pl.pallas_call(
        finish,
        out_shape=(
            jax.ShapeDtypeStruct((units, rows_half), bf16),
            jax.ShapeDtypeStruct((units, rows_half), bf16),
            jax.ShapeDtypeStruct((3, 8, rows_half), f32),
        ),
        grid_spec=pltpu.PrefetchScalarGridSpec(
            num_scalar_prefetch=1,
            grid=(units // chunk,),
            in_specs=[
                pl.BlockSpec((per_core, 2, chunk, local_rows), lambda u, ids: (0, 0, u, 0)),
                pl.BlockSpec((per_core, 2, chunk, local_rows), lambda u, ids: (0, 0, u, 0)),
                pl.BlockSpec((dp_count, tp_count * ranks, chunk), lambda u, ids: (0, 0, u)),
                pl.BlockSpec((rows_half, tp_count * ranks), lambda u, ids: (0, 0)),
            ],
            out_specs=[
                pl.BlockSpec((chunk, rows_half), lambda u, ids: (u, 0)),
                pl.BlockSpec((chunk, rows_half), lambda u, ids: (u, 0)),
                pl.BlockSpec((3, 8, rows_half), lambda u, ids: (0, 0, 0)),
            ],
        ),
        compiler_params=pltpu.CompilerParams(vmem_limit_bytes=60 * 1024 * 1024),
        name="finish",
    )(own_ids, own, peer, adapters, own_down)
    seg_count = live_rows.shape[0]
    spread = jnp.zeros((8, total_rows), f32).at[:seg_count].set(live_rows.astype(f32))
    own_live = lax.dynamic_slice_in_dim(spread, tp_index * rows_half, rows_half, 1)
    seg_sums = pl.pallas_call(
        functools.partial(divergence, dp_count),
        out_shape=jax.ShapeDtypeStruct((8, 128), f32),
        in_specs=[vmem_spec] * 2,
        out_specs=vmem_spec,
        scratch_shapes=[
            pltpu.VMEM((8, rows_half), f32),
            pltpu.VMEM((dp_count, 8, rows_half), f32),
            pltpu.VMEM((2, 8, 128), f32),
            dma((dp_count,)), dma((dp_count,)),
        ],
        compiler_params=pltpu.CompilerParams(collective_id=1, has_side_effects=True),
        name="divergence",
    )(sums, own_live)
    seg_kl = seg_sums[:seg_count, 0] / counts
    return (ref_hidden, pol_hidden, seg_kl)


def pick_shards(*args):
    rows = args[0].shape[0]
    units = args[1].shape[0]
    sizes = (lax.axis_size("groups"), lax.axis_size("tensor"))
    fits = rows == BLOCK and units % 256 == 0 and sizes == (2, 2) and lax.axis_size("dp") == 8
    return kernel_shards(*args) if fits else shards(*args)


def solution(mesh):
    in_specs = (
        P(("groups", "dp"), "tensor"),
        P("dp", "tensor"),
        P("dp", "tensor"),
        P("dp", "tensor", None),
        P("dp", "tensor", None),
        P("groups"),
        P("groups"),
        P("groups"),
    )
    out_specs = (P("dp", ("groups", "tensor")), P("dp", ("groups", "tensor")), P("groups"))
    return jax.shard_map(pick_shards, mesh=mesh, in_specs=in_specs, out_specs=out_specs, check_vma=False)
```

```python
import functools
import jax
import jax.numpy as jnp
from jax import lax
from jax.experimental import pallas as pl
from jax.experimental.pallas import tpu as pltpu
from jax.sharding import PartitionSpec as P

BLOCK = 128


def spread_2(value, axis, root):
    mine = lax.axis_index(axis) == root
    return lax.psum(jnp.where(mine, value, jnp.zeros_like(value)), axis)


def segment_tables(segment_block_counts, segment_live_rows, total_rows):
    order = jnp.arange(segment_block_counts.shape[0])
    before = order[None, :] <= order[:, None]
    seg_ends = jnp.sum(jnp.where(before, segment_block_counts[None, :], 0), axis=1)
    starts = seg_ends - segment_block_counts
    row_ids = jnp.arange(total_rows, dtype=jnp.int32)
    blocks = row_ids // BLOCK
    member = (blocks[None, :] >= starts[:, None]) & (blocks[None, :] < seg_ends[:, None])
    live_limit = (seg_ends - 1) * BLOCK + segment_live_rows
    live_rows = member & (row_ids[None, :] < live_limit[:, None])
    counts = (live_limit - starts * BLOCK).astype(jnp.float32)
    return (member, live_rows, counts)


def project_tokens(tokens, gate_weight_base, up_weight_base, adapter_down_matrix, owned_rows):
    contract = (((1,), (1,)), ((), ()))
    rank_pair = adapter_down_matrix.shape[1]
    block_rows = lax.all_gather(tokens, "dp", axis=0, tiled=True)
    row_count = block_rows.shape[0]
    gate_part = lax.dot_general(
        gate_weight_base, block_rows, contract, preferred_element_type=jnp.float32
    )
    up_part = lax.dot_general(
        up_weight_base, block_rows, contract, preferred_element_type=jnp.float32
    )
    base_terms = jnp.stack([gate_part, up_part])
    contrib = lax.cond(
        jnp.any(owned_rows),
        lambda: jnp.dot(block_rows, adapter_down_matrix, preferred_element_type=jnp.float32)
        * owned_rows[:, None].astype(jnp.float32),
        lambda: jnp.zeros((row_count, rank_pair), jnp.float32),
    )
    return (base_terms, contrib)


def shards(
    tokens,
    gate_weight_base,
    up_weight_base,
    adapter_down_stack,
    adapter_up_stack,
    segment_block_counts,
    segment_adapter_ids,
    segment_live_rows,
):
    dp_count = lax.axis_size("dp")
    tp_count = lax.axis_size("tensor")
    dp_index = lax.axis_index("dp")
    tp_index = lax.axis_index("tensor")
    local_rows = tokens.shape[0]
    total_rows = local_rows * dp_count
    rows_half = total_rows // tp_count
    seg_count = segment_block_counts.shape[0]
    member, live_rows, counts = segment_tables(segment_block_counts, segment_live_rows, total_rows)
    adapter_down_matrix = adapter_down_stack[0]
    rank_pair = adapter_down_matrix.shape[1]
    base_terms, unused_terms = project_tokens(
        tokens,
        gate_weight_base,
        up_weight_base,
        adapter_down_matrix,
        jnp.zeros((total_rows,), jnp.bool_),
    )
    home_first = dp_index * local_rows
    home_member = lax.dynamic_slice_in_dim(member, home_first, local_rows, 1).astype(jnp.float32)

    def fetch_slot(buffer_slot, accum):
        fetched = spread_2(adapter_down_matrix, "dp", segment_adapter_ids[buffer_slot])
        return (
            accum
            + jnp.dot(tokens, fetched, preferred_element_type=jnp.float32)
            * home_member[buffer_slot][:, None]
        )

    home_terms = lax.fori_loop(
        0, seg_count, fetch_slot, jnp.zeros((local_rows, rank_pair), jnp.float32)
    )
    down_terms = lax.dynamic_update_slice_in_dim(
        jnp.zeros((total_rows, rank_pair), jnp.float32), home_terms, home_first, 0
    )
    down_proj = lax.psum(down_terms, ("dp", "tensor")).astype(jnp.bfloat16)
    slice_list = lax.all_to_all(adapter_up_stack, "dp", split_axis=2, concat_axis=0, tiled=True)
    adapters = slice_list.shape[0]
    rank_part = slice_list.shape[1]
    ff_dev = slice_list.shape[2]
    picker = (
        segment_adapter_ids[:, None] == jnp.arange(adapters, dtype=jnp.int32)[None, :]
    ).astype(jnp.bfloat16)
    chosen = jnp.einsum(
        "sa,aqf->sqf", picker, slice_list, preferred_element_type=jnp.float32
    ).astype(jnp.bfloat16)
    own_ranks = lax.dynamic_slice_in_dim(down_proj, tp_index * rank_part, rank_part, 1)
    spread = (member.T.astype(jnp.bfloat16)[:, :, None] * own_ranks[:, None, :]).reshape(
        total_rows, seg_count * rank_part
    )
    delta_cols = lax.dot_general(
        chosen.reshape(seg_count * rank_part, ff_dev),
        spread,
        (((0,), (1,)), ((), ())),
        preferred_element_type=jnp.float32,
    )
    upper = tp_index >= tp_count // 2
    blank = jnp.zeros_like(delta_cols)
    policy_terms = base_terms + jnp.stack(
        [jnp.where(upper, blank, delta_cols), jnp.where(upper, delta_cols, blank)]
    )
    halves = lax.psum_scatter(
        jnp.stack([base_terms, policy_terms]), "tensor", scatter_dimension=3, tiled=True
    )
    ref_hidden = (jax.nn.silu(halves[0, 0]) * halves[0, 1]).astype(jnp.bfloat16)
    pol_hidden = (jax.nn.silu(halves[1, 0]) * halves[1, 1]).astype(jnp.bfloat16)
    ref_vals = 4.0 * jnp.tanh(ref_hidden.astype(jnp.float32) * 0.25)
    pol_vals = 4.0 * jnp.tanh(pol_hidden.astype(jnp.float32) * 0.25)
    pol_exp = jnp.exp(pol_vals)
    first_half = tp_index * rows_half

    def placed(values):
        return lax.dynamic_update_slice_in_dim(
            jnp.zeros((total_rows,), jnp.float32), values, first_half, 0
        )

    ref_sum, pol_sum, cross_sum = lax.psum(
        (
            placed(jnp.sum(jnp.exp(ref_vals), axis=0)),
            placed(jnp.sum(pol_exp, axis=0)),
            placed(jnp.sum(pol_exp * (pol_vals - ref_vals), axis=0)),
        ),
        ("dp", "tensor"),
    )
    kl_row = cross_sum / pol_sum - jnp.log(pol_sum) + jnp.log(ref_sum)
    seg_kl = jnp.sum(live_rows.astype(jnp.float32) * kl_row[None, :], axis=1) / counts
    return (ref_hidden, pol_hidden, seg_kl)


MESH = pl.DeviceIdType.MESH


def ring_place(dp_index, count):
    odd = dp_index % 2
    return odd * (count - 1 - dp_index // 2) + (1 - odd) * (dp_index // 2)


def ring_index(place, count):
    upper = place // (count // 2)
    return (1 - upper) * 2 * place + upper * (2 * (count - 1 - place) + 1)


def gather_project(
    dp_count, tp_count, group_count, unit_chunk,
    tokens, gate, up, down, adapter_up, owned,
    own_out, peer_out, adapters_out, down_out,
    tok_buf, weights, down_buf, parts, contrib, contrib_peer, published, heard, reduced, gathered,
    load_sem, ring_send, ring_recv, ad_send, ad_recv, pass_send, pass_recv,
    part_send, part_recv, con_send, con_recv, pub_send, pub_recv,
    red_send, red_recv, cross_send, cross_recv,
):
    half = dp_count // 2
    rows = tokens.shape[0]
    units = gate.shape[0]
    ranks = adapter_up.shape[0]
    me = lax.axis_index("dp")
    core = lax.axis_index("tensor")
    group = lax.axis_index("groups")
    place = ring_place(me, dp_count)
    right = ring_index((place + 1) % dp_count, dp_count)
    left = ring_index((place + dp_count - 1) % dp_count, dp_count)
    other_core = 1 - core
    other_group = 1 - group

    barrier = pltpu.get_barrier_semaphore()
    for k in range(1, dp_count):
        pl.semaphore_signal(barrier, inc=1, device_id={"dp": (me + k) % dp_count}, device_id_type=MESH)
    pl.semaphore_signal(barrier, inc=1, device_id={"tensor": other_core}, device_id_type=MESH)
    pl.semaphore_signal(barrier, inc=1, device_id={"groups": other_group}, device_id_type=MESH)
    pl.semaphore_wait(barrier, dp_count + 1)

    def block(slot):
        return tok_buf.at[pl.ds(slot * rows, rows)]

    def plan(src, dst, sem, axis, target, sends, recvs):
        return pltpu.make_async_remote_copy(
            src_ref=src, dst_ref=dst, send_sem=sends.at[sem], recv_sem=recvs.at[sem],
            device_id={axis: target}, device_id_type=MESH,
        )

    def send(*where):
        copy = plan(*where)
        copy.start()
        return copy

    def inside(place_value):
        return (place_value % half) * (half - 1 - place_value % half) > 0

    across = ring_index(dp_count - 1 - place, dp_count)
    middle = inside(place)
    right_end = jnp.logical_not(inside((place + 1) % dp_count))
    left_end = jnp.logical_not(inside((place + dp_count - 1) % dp_count))

    last = dp_count - 1
    cut = rows // 2
    cw = send(tokens, block(1), 0, "dp", right, ring_send, ring_recv)
    ccw = send(tokens, block(2), 1, "dp", left, ring_send, ring_recv)

    loads = [
        pltpu.make_async_copy(tokens, block(0), load_sem.at[0]),
        pltpu.make_async_copy(gate, weights.at[0], load_sem.at[1]),
        pltpu.make_async_copy(up, weights.at[1], load_sem.at[2]),
        pltpu.make_async_copy(down, down_buf, load_sem.at[3]),
    ]
    for load in loads:
        load.start()

    share = ranks // group_count
    mine = pl.ds(pl.multiple_of(group * share, 16), share)
    landing = pl.ds(pl.multiple_of(core * ranks + group * share, 16), share)
    ad_copies = []
    for k in range(1, dp_count):
        target = (me + k) % dp_count
        ad_copies.append(send(
            adapter_up.at[mine, pl.ds(pl.multiple_of(target * units, 128), units)],
            adapters_out.at[me, landing], k, "dp", target, ad_send, ad_recv,
        ))
    ad_local = pltpu.make_async_copy(
        adapter_up.at[mine, pl.ds(pl.multiple_of(me * units, 128), units)],
        adapters_out.at[me, landing], load_sem.at[4],
    )
    ad_local.start()
    for load in loads:
        load.wait()

    def project(slot, blocks, matrices=(0, 2)):
        def chunk(step, carry):
            which = step // (units // unit_chunk)
            first = pl.multiple_of((step % (units // unit_chunk)) * unit_chunk, unit_chunk)
            value = lax.dot_general(
                weights[which, pl.ds(first, unit_chunk), :],
                tok_buf[pl.ds(slot * rows, blocks * rows), :],
                (((1,), (1,)), ((), ())), preferred_element_type=jnp.float32,
            )
            for b in range(blocks):
                parts[slot + b, which, pl.ds(first, unit_chunk), :] = value[:, b * rows:(b + 1) * rows]
            return carry

        per_matrix = units // unit_chunk
        lax.fori_loop(matrices[0] * per_matrix, matrices[1] * per_matrix, chunk, 0)

    def project_down(slot, blocks):
        contrib[pl.ds(slot * rows, blocks * rows), :] = jnp.dot(
            tok_buf[pl.ds(slot * rows, blocks * rows), :], down_buf[...],
            preferred_element_type=jnp.float32,
        )
        for j in range(slot, slot + blocks):
            @pl.when(slot_block[j] // per_core != core)
            def _():
                contrib_copy(j).start()

    per_core = dp_count // tp_count
    slot_place = [place]
    for s in range(1, half):
        slot_place += [(place + dp_count - s) % dp_count, (place + s) % dp_count]
    slot_place.append((place + half) % dp_count)
    slot_block = [ring_index(q, dp_count) for q in slot_place]

    def part_copy(slot):
        where = slot_block[slot] % per_core
        return pltpu.make_async_remote_copy(
            src_ref=parts.at[slot], dst_ref=peer_out.at[where],
            send_sem=part_send.at[slot], recv_sem=part_recv.at[where],
            device_id={"tensor": other_core}, device_id_type=MESH,
        )

    def own_copy(slot):
        where = slot_block[slot] % per_core
        return pltpu.make_async_copy(parts.at[slot], own_out.at[where], part_send.at[slot])

    def contrib_copy(slot):
        where = slot_block[slot] % per_core
        return pltpu.make_async_remote_copy(
            src_ref=contrib.at[pl.ds(slot * rows, rows)], dst_ref=contrib_peer.at[where],
            send_sem=con_send.at[slot], recv_sem=con_recv.at[where],
            device_id={"tensor": other_core}, device_id_type=MESH,
        )

    strip = rows // dp_count

    def publish_copy(where, k):
        target = (me + k) % dp_count
        return pltpu.make_async_remote_copy(
            src_ref=published.at[where, pl.ds(pl.multiple_of(target * strip, 16), strip)],
            dst_ref=heard.at[k - 1, where],
            send_sem=pub_send.at[k - 1, where], recv_sem=pub_recv.at[k - 1, where],
            device_id={"dp": (me + k) % dp_count}, device_id_type=MESH,
        )

    def publish(slot):
        where = slot_block[slot] % per_core

        @pl.when(slot_block[slot] // per_core == core)
        def _():
            contrib_copy(slot).wait_recv()
            total = contrib[pl.ds(slot * rows, rows), :] + contrib_peer[where]
            published[where] = (total * owned[slot_block[slot], 0:1, :]).astype(published.dtype)
            for k in range(1, dp_count):
                publish_copy(where, k).start()

    def hand_over(slot):
        @pl.when(slot_block[slot] // per_core == core)
        def _():
            own_copy(slot).start()

        @pl.when(slot_block[slot] // per_core != core)
        def _():
            part_copy(slot).start()

    project_down(0, 1)
    project(0, 1)
    hand_over(0)
    publish(0)
    sent = [cw, ccw]
    passes = []
    for s in range(1, half):
        cw.wait_recv()
        ccw.wait_recv()
        if s < half - 1:
            cw = send(block(2 * s - 1), block(2 * s + 1), 2 * s, "dp", right, ring_send, ring_recv)
            ccw = send(block(2 * s), block(2 * s + 2), 2 * s + 1, "dp", left, ring_send, ring_recv)
        else:
            a, b = (2 * s - 1) * rows, 2 * s * rows + cut
            z = last * rows
            last_cw = plan(tok_buf.at[pl.ds(a, cut)], tok_buf.at[pl.ds(z, cut)],
                           2 * s, "dp", right, ring_send, ring_recv)
            last_ccw = plan(tok_buf.at[pl.ds(b, cut)], tok_buf.at[pl.ds(z + cut, cut)],
                            2 * s + 1, "dp", left, ring_send, ring_recv)
            pl.when(right_end)(last_cw.start)
            pl.when(left_end)(last_ccw.start)
        if s < half - 1:
            sent += [cw, ccw]
        if s == 1:
            source = pl.multiple_of((1 + place % 2) * rows, rows)
            crossing = plan(tok_buf.at[pl.ds(source, rows)], block(last),
                            0, "dp", across, cross_send, cross_recv)
            pl.when(middle)(crossing.start)
        project_down(2 * s - 1, 2)
        project(2 * s - 1, 2)
        hand_over(2 * s - 1)
        hand_over(2 * s)
        publish(2 * s - 1)
        publish(2 * s)
        if s == half - 2:
            for copy in ad_copies:
                copy.wait_recv()
            ad_local.wait()
            region = adapters_out.at[:, landing]
            passes.append(send(region, region, 0, "groups", other_group, pass_send, pass_recv))
        if s == half - 1:
            passes[0].wait_recv()
            region = adapters_out.at[:, pl.ds(pl.multiple_of(core * ranks, 16), ranks)]
            passes.append(send(region, region, 1, "tensor", other_core, pass_send, pass_recv))

    @pl.when(middle)
    def _():
        crossing.wait_recv()
        crossing.wait_send()

    @pl.when(jnp.logical_not(middle))
    def _():
        last_cw.wait_recv()
        last_ccw.wait_recv()

    project_down(last, 1)
    publish(last)
    project(last, 1, (0, 1))
    for where in range(per_core):
        for k in range(1, dp_count):
            publish_copy(where, k).wait_recv()
        total = published[where, pl.ds(pl.multiple_of(me * strip, 16), strip), :].astype(jnp.float32)
        for k in range(1, dp_count):
            total = total + heard[k - 1, where].astype(jnp.float32)
        reduced[where] = total.astype(reduced.dtype)
    spreads = []
    for k in range(1, dp_count):
        spreads.append(send(
            reduced, gathered.at[me], k, "dp", (me + k) % dp_count, red_send, red_recv
        ))
    project(last, 1, (1, 2))
    hand_over(last)
    for copy in spreads:
        copy.wait_recv()
    gathered[me] = reduced[...]
    for where in range(per_core):
        for d in range(dp_count):
            down_out[pl.ds(where * rows + d * strip, strip), :] = gathered[d, where]

    pl.when(right_end)(last_cw.wait_send)
    pl.when(left_end)(last_ccw.wait_send)
    for copy in sent + ad_copies + passes + spreads:
        copy.wait_send()
    passes[1].wait_recv()
    for slot in range(dp_count):
        @pl.when(slot_block[slot] // per_core == core)
        def _():
            own_copy(slot).wait()

        @pl.when(slot_block[slot] // per_core != core)
        def _():
            part_copy(slot).wait_send()
            contrib_copy(slot).wait_send()

    for where in range(per_core):
        for k in range(1, dp_count):
            publish_copy(where, k).wait_send()
        pltpu.make_async_remote_copy(
            src_ref=parts.at[where], dst_ref=peer_out.at[where],
            send_sem=part_send.at[where], recv_sem=part_recv.at[where],
            device_id={"tensor": other_core}, device_id_type=MESH,
        ).wait_recv()


def finish(ids, own, peer, adapters, down_proj, ref_out, pol_out, sums):
    blocks = own.shape[0]
    rows = own.shape[3]
    ranks = down_proj.shape[1] // 2

    @pl.when(pl.program_id(0) == 0)
    def _():
        sums[...] = jnp.zeros_like(sums)

    def silu(v):
        return v / (1.0 + jnp.exp(-v))

    contract = (((0,), (1,)), ((), ()))
    for j in range(blocks):
        columns = slice(j * rows, (j + 1) * rows)
        gate = own[j, 0] + peer[j, 0]
        up = own[j, 1] + peer[j, 1]
        chosen = adapters[ids[j]]
        ref_hidden = (silu(gate) * up).astype(jnp.bfloat16)
        ref_out[:, columns] = ref_hidden
        gate = gate + lax.dot_general(
            chosen[:ranks], down_proj[columns, :ranks], contract, preferred_element_type=jnp.float32
        )
        up = up + lax.dot_general(
            chosen[ranks:], down_proj[columns, ranks:], contract, preferred_element_type=jnp.float32
        )
        pol_hidden = (silu(gate) * up).astype(jnp.bfloat16)
        pol_out[:, columns] = pol_hidden
        ref_vals = 4.0 * jnp.tanh(ref_hidden.astype(jnp.float32) * 0.25)
        pol_vals = 4.0 * jnp.tanh(pol_hidden.astype(jnp.float32) * 0.25)
        pol_exp = jnp.exp(pol_vals)
        for k, value in enumerate((jnp.exp(ref_vals), pol_exp, pol_exp * (pol_vals - ref_vals))):
            sums[k, :, columns] += value.reshape(-1, 8, rows).sum(axis=0)


def divergence(dp_count, sums, live, out, mine, heard, halves, send_sem, recv_sem):
    me = lax.axis_index("dp")
    other_core = 1 - lax.axis_index("tensor")
    barrier = pltpu.get_barrier_semaphore()
    for k in range(1, dp_count):
        pl.semaphore_signal(barrier, inc=1, device_id={"dp": (me + k) % dp_count}, device_id_type=MESH)
    pl.semaphore_signal(barrier, inc=1, device_id={"tensor": other_core}, device_id_type=MESH)
    for k in range(3):
        mine[k:k + 1, :] = jnp.sum(sums[k], axis=0, keepdims=True)
    mine[3:8, :] = jnp.zeros((5, mine.shape[1]), jnp.float32)
    pl.semaphore_wait(barrier, dp_count)
    copies = []
    for k in range(1, dp_count):
        copies.append(pltpu.make_async_remote_copy(
            src_ref=mine, dst_ref=heard.at[me], send_sem=send_sem.at[k], recv_sem=recv_sem.at[k],
            device_id={"dp": (me + k) % dp_count}, device_id_type=MESH,
        ))
        copies[-1].start()
    for copy in copies:
        copy.wait_recv()
    heard[me] = mine[...]
    total = heard[0]
    for k in range(1, dp_count):
        total = total + heard[k]
    ref_sum, pol_sum, cross_sum = total[0:1], total[1:2], total[2:3]
    kl_row = cross_sum / pol_sum - jnp.log(pol_sum) + jnp.log(ref_sum)
    part = jnp.sum(live[...] * kl_row, axis=1, keepdims=True)
    halves[0] = jnp.broadcast_to(part, (8, 128))
    swap = pltpu.make_async_remote_copy(
        src_ref=halves.at[0], dst_ref=halves.at[1], send_sem=send_sem.at[0], recv_sem=recv_sem.at[0],
        device_id={"tensor": other_core}, device_id_type=MESH,
    )
    swap.start()
    swap.wait()
    for copy in copies:
        copy.wait_send()
    out[...] = halves[0] + halves[1]


def kernel_shards(
    tokens, gate_weight_base, up_weight_base, adapter_down_stack, adapter_up_stack,
    segment_block_counts, segment_adapter_ids, segment_live_rows,
):
    dp_count = lax.axis_size("dp")
    tp_count = lax.axis_size("tensor")
    group_count = lax.axis_size("groups")
    dp_index = lax.axis_index("dp")
    tp_index = lax.axis_index("tensor")
    local_rows, features = tokens.shape
    units = gate_weight_base.shape[0]
    ranks = adapter_up_stack.shape[1]
    total_rows = local_rows * dp_count
    per_core = dp_count // tp_count
    rows_half = total_rows // tp_count
    member, live_rows, counts = segment_tables(segment_block_counts, segment_live_rows, total_rows)
    row_adapter = jnp.sum(member.astype(jnp.int32) * segment_adapter_ids[:, None], axis=0)
    f32, bf16 = jnp.float32, jnp.bfloat16
    any_spec = pl.BlockSpec(memory_space=pl.ANY)
    dma = pltpu.SemaphoreType.DMA
    owned = jnp.broadcast_to(
        (row_adapter[::local_rows] == dp_index).astype(f32)[:, None, None],
        (dp_count, 8, tp_count * ranks),
    )
    vmem_spec = pl.BlockSpec(memory_space=pltpu.VMEM)
    own, peer, adapters, own_down = pl.pallas_call(
        functools.partial(gather_project, dp_count, tp_count, group_count, units // 2),
        out_shape=(
            jax.ShapeDtypeStruct((per_core, 2, units, local_rows), f32),
            jax.ShapeDtypeStruct((per_core, 2, units, local_rows), f32),
            jax.ShapeDtypeStruct((dp_count, tp_count * ranks, units), bf16),
            jax.ShapeDtypeStruct((rows_half, tp_count * ranks), bf16),
        ),
        in_specs=[any_spec] * 5 + [vmem_spec],
        out_specs=(any_spec,) * 3 + (vmem_spec,),
        scratch_shapes=[
            pltpu.VMEM((total_rows, features), bf16),
            pltpu.VMEM((2, units, features), bf16),
            pltpu.VMEM((features, tp_count * ranks), bf16),
            pltpu.VMEM((dp_count, 2, units, local_rows), f32),
            pltpu.VMEM((total_rows, tp_count * ranks), f32),
            pltpu.VMEM((per_core, local_rows, tp_count * ranks), f32),
            pltpu.VMEM((per_core, local_rows, tp_count * ranks), bf16),
            pltpu.VMEM((dp_count - 1, per_core, local_rows // dp_count, tp_count * ranks), bf16),
            pltpu.VMEM((per_core, local_rows // dp_count, tp_count * ranks), bf16),
            pltpu.VMEM((dp_count, per_core, local_rows // dp_count, tp_count * ranks), bf16),
            dma((5,)), dma((dp_count,)), dma((dp_count,)), dma((dp_count,)), dma((dp_count,)),
            dma((2,)), dma((2,)), dma((dp_count,)), dma((per_core,)), dma((dp_count,)), dma((per_core,)),
            dma((dp_count - 1, per_core)), dma((dp_count - 1, per_core)), dma((dp_count,)), dma((dp_count,)),
            dma((1,)), dma((1,)),
        ],
        compiler_params=pltpu.CompilerParams(
            collective_id=0, has_side_effects=True, vmem_limit_bytes=60 * 1024 * 1024
        ),
        name="gather_project",
    )(tokens, gate_weight_base, up_weight_base, adapter_down_stack[0], adapter_up_stack[0], owned)
    own_ids = lax.dynamic_slice_in_dim(row_adapter[::local_rows], tp_index * per_core, per_core, 0)
    chunk = 256
    ref_hidden, pol_hidden, sums = pl.pallas_call(
        finish,
        out_shape=(
            jax.ShapeDtypeStruct((units, rows_half), bf16),
            jax.ShapeDtypeStruct((units, rows_half), bf16),
            jax.ShapeDtypeStruct((3, 8, rows_half), f32),
        ),
        grid_spec=pltpu.PrefetchScalarGridSpec(
            num_scalar_prefetch=1,
            grid=(units // chunk,),
            in_specs=[
                pl.BlockSpec((per_core, 2, chunk, local_rows), lambda u, ids: (0, 0, u, 0)),
                pl.BlockSpec((per_core, 2, chunk, local_rows), lambda u, ids: (0, 0, u, 0)),
                pl.BlockSpec((dp_count, tp_count * ranks, chunk), lambda u, ids: (0, 0, u)),
                pl.BlockSpec((rows_half, tp_count * ranks), lambda u, ids: (0, 0)),
            ],
            out_specs=[
                pl.BlockSpec((chunk, rows_half), lambda u, ids: (u, 0)),
                pl.BlockSpec((chunk, rows_half), lambda u, ids: (u, 0)),
                pl.BlockSpec((3, 8, rows_half), lambda u, ids: (0, 0, 0)),
            ],
        ),
        compiler_params=pltpu.CompilerParams(vmem_limit_bytes=60 * 1024 * 1024),
        name="finish",
    )(own_ids, own, peer, adapters, own_down)
    seg_count = live_rows.shape[0]
    spread = jnp.zeros((8, total_rows), f32).at[:seg_count].set(live_rows.astype(f32))
    own_live = lax.dynamic_slice_in_dim(spread, tp_index * rows_half, rows_half, 1)
    seg_sums = pl.pallas_call(
        functools.partial(divergence, dp_count),
        out_shape=jax.ShapeDtypeStruct((8, 128), f32),
        in_specs=[vmem_spec] * 2,
        out_specs=vmem_spec,
        scratch_shapes=[
            pltpu.VMEM((8, rows_half), f32),
            pltpu.VMEM((dp_count, 8, rows_half), f32),
            pltpu.VMEM((2, 8, 128), f32),
            dma((dp_count,)), dma((dp_count,)),
        ],
        compiler_params=pltpu.CompilerParams(collective_id=1, has_side_effects=True),
        name="divergence",
    )(sums, own_live)
    seg_kl = seg_sums[:seg_count, 0] / counts
    return (ref_hidden, pol_hidden, seg_kl)


def pick_shards(*args):
    rows = args[0].shape[0]
    units = args[1].shape[0]
    sizes = (lax.axis_size("groups"), lax.axis_size("tensor"))
    fits = rows == BLOCK and units % 256 == 0 and sizes == (2, 2) and lax.axis_size("dp") == 8
    return kernel_shards(*args) if fits else shards(*args)


def solution(mesh):
    in_specs = (
        P(("groups", "dp"), "tensor"),
        P("dp", "tensor"),
        P("dp", "tensor"),
        P("dp", "tensor", None),
        P("dp", "tensor", None),
        P("groups"),
        P("groups"),
        P("groups"),
    )
    out_specs = (P("dp", ("groups", "tensor")), P("dp", ("groups", "tensor")), P("groups"))
    return jax.shard_map(pick_shards, mesh=mesh, in_specs=in_specs, out_specs=out_specs, check_vma=False)
```

```python
import functools
import jax
import jax.numpy as jnp
from jax import lax
from jax.experimental import pallas as pl
from jax.experimental.pallas import tpu as pltpu
from jax.sharding import PartitionSpec as P

BLOCK = 128


def spread_2(value, axis, root):
    mine = lax.axis_index(axis) == root
    return lax.psum(jnp.where(mine, value, jnp.zeros_like(value)), axis)


def segment_tables(segment_block_counts, segment_live_rows, total_rows):
    order = jnp.arange(segment_block_counts.shape[0])
    before = order[None, :] <= order[:, None]
    seg_ends = jnp.sum(jnp.where(before, segment_block_counts[None, :], 0), axis=1)
    starts = seg_ends - segment_block_counts
    row_ids = jnp.arange(total_rows, dtype=jnp.int32)
    blocks = row_ids // BLOCK
    member = (blocks[None, :] >= starts[:, None]) & (blocks[None, :] < seg_ends[:, None])
    live_limit = (seg_ends - 1) * BLOCK + segment_live_rows
    live_rows = member & (row_ids[None, :] < live_limit[:, None])
    counts = (live_limit - starts * BLOCK).astype(jnp.float32)
    return (member, live_rows, counts)


def project_tokens(tokens, gate_weight_base, up_weight_base, adapter_down_matrix, owned_rows):
    contract = (((1,), (1,)), ((), ()))
    rank_pair = adapter_down_matrix.shape[1]
    block_rows = lax.all_gather(tokens, "dp", axis=0, tiled=True)
    row_count = block_rows.shape[0]
    gate_part = lax.dot_general(
        gate_weight_base, block_rows, contract, preferred_element_type=jnp.float32
    )
    up_part = lax.dot_general(
        up_weight_base, block_rows, contract, preferred_element_type=jnp.float32
    )
    base_terms = jnp.stack([gate_part, up_part])
    contrib = lax.cond(
        jnp.any(owned_rows),
        lambda: jnp.dot(block_rows, adapter_down_matrix, preferred_element_type=jnp.float32)
        * owned_rows[:, None].astype(jnp.float32),
        lambda: jnp.zeros((row_count, rank_pair), jnp.float32),
    )
    return (base_terms, contrib)


def shards(
    tokens,
    gate_weight_base,
    up_weight_base,
    adapter_down_stack,
    adapter_up_stack,
    segment_block_counts,
    segment_adapter_ids,
    segment_live_rows,
):
    dp_count = lax.axis_size("dp")
    tp_count = lax.axis_size("tensor")
    dp_index = lax.axis_index("dp")
    tp_index = lax.axis_index("tensor")
    local_rows = tokens.shape[0]
    total_rows = local_rows * dp_count
    rows_half = total_rows // tp_count
    seg_count = segment_block_counts.shape[0]
    member, live_rows, counts = segment_tables(segment_block_counts, segment_live_rows, total_rows)
    adapter_down_matrix = adapter_down_stack[0]
    rank_pair = adapter_down_matrix.shape[1]
    base_terms, unused_terms = project_tokens(
        tokens,
        gate_weight_base,
        up_weight_base,
        adapter_down_matrix,
        jnp.zeros((total_rows,), jnp.bool_),
    )
    home_first = dp_index * local_rows
    home_member = lax.dynamic_slice_in_dim(member, home_first, local_rows, 1).astype(jnp.float32)

    def fetch_slot(buffer_slot, accum):
        fetched = spread_2(adapter_down_matrix, "dp", segment_adapter_ids[buffer_slot])
        return (
            accum
            + jnp.dot(tokens, fetched, preferred_element_type=jnp.float32)
            * home_member[buffer_slot][:, None]
        )

    home_terms = lax.fori_loop(
        0, seg_count, fetch_slot, jnp.zeros((local_rows, rank_pair), jnp.float32)
    )
    down_terms = lax.dynamic_update_slice_in_dim(
        jnp.zeros((total_rows, rank_pair), jnp.float32), home_terms, home_first, 0
    )
    down_proj = lax.psum(down_terms, ("dp", "tensor")).astype(jnp.bfloat16)
    slice_list = lax.all_to_all(adapter_up_stack, "dp", split_axis=2, concat_axis=0, tiled=True)
    adapters = slice_list.shape[0]
    rank_part = slice_list.shape[1]
    ff_dev = slice_list.shape[2]
    picker = (
        segment_adapter_ids[:, None] == jnp.arange(adapters, dtype=jnp.int32)[None, :]
    ).astype(jnp.bfloat16)
    chosen = jnp.einsum(
        "sa,aqf->sqf", picker, slice_list, preferred_element_type=jnp.float32
    ).astype(jnp.bfloat16)
    own_ranks = lax.dynamic_slice_in_dim(down_proj, tp_index * rank_part, rank_part, 1)
    spread = (member.T.astype(jnp.bfloat16)[:, :, None] * own_ranks[:, None, :]).reshape(
        total_rows, seg_count * rank_part
    )
    delta_cols = lax.dot_general(
        chosen.reshape(seg_count * rank_part, ff_dev),
        spread,
        (((0,), (1,)), ((), ())),
        preferred_element_type=jnp.float32,
    )
    upper = tp_index >= tp_count // 2
    blank = jnp.zeros_like(delta_cols)
    policy_terms = base_terms + jnp.stack(
        [jnp.where(upper, blank, delta_cols), jnp.where(upper, delta_cols, blank)]
    )
    halves = lax.psum_scatter(
        jnp.stack([base_terms, policy_terms]), "tensor", scatter_dimension=3, tiled=True
    )
    ref_hidden = (jax.nn.silu(halves[0, 0]) * halves[0, 1]).astype(jnp.bfloat16)
    pol_hidden = (jax.nn.silu(halves[1, 0]) * halves[1, 1]).astype(jnp.bfloat16)
    ref_vals = 4.0 * jnp.tanh(ref_hidden.astype(jnp.float32) * 0.25)
    pol_vals = 4.0 * jnp.tanh(pol_hidden.astype(jnp.float32) * 0.25)
    pol_exp = jnp.exp(pol_vals)
    first_half = tp_index * rows_half

    def placed(values):
        return lax.dynamic_update_slice_in_dim(
            jnp.zeros((total_rows,), jnp.float32), values, first_half, 0
        )

    ref_sum, pol_sum, cross_sum = lax.psum(
        (
            placed(jnp.sum(jnp.exp(ref_vals), axis=0)),
            placed(jnp.sum(pol_exp, axis=0)),
            placed(jnp.sum(pol_exp * (pol_vals - ref_vals), axis=0)),
        ),
        ("dp", "tensor"),
    )
    kl_row = cross_sum / pol_sum - jnp.log(pol_sum) + jnp.log(ref_sum)
    seg_kl = jnp.sum(live_rows.astype(jnp.float32) * kl_row[None, :], axis=1) / counts
    return (ref_hidden, pol_hidden, seg_kl)


MESH = pl.DeviceIdType.MESH


def ring_place(dp_index, count):
    odd = dp_index % 2
    return odd * (count - 1 - dp_index // 2) + (1 - odd) * (dp_index // 2)


def ring_index(place, count):
    upper = place // (count // 2)
    return (1 - upper) * 2 * place + upper * (2 * (count - 1 - place) + 1)


def gather_project(
    dp_count, tp_count, group_count, unit_chunk,
    tokens, gate, up, down, adapter_up, owned,
    own_out, peer_out, adapters_out, down_out,
    tok_buf, weights, down_buf, parts, contrib, contrib_peer, published, heard, reduced, gathered,
    load_sem, ring_send, ring_recv, ad_send, ad_recv, pass_send, pass_recv,
    part_send, part_recv, con_send, con_recv, pub_send, pub_recv,
    red_send, red_recv, cross_send, cross_recv,
):
    half = dp_count // 2
    rows = tokens.shape[0]
    units = gate.shape[0]
    ranks = adapter_up.shape[0]
    me = lax.axis_index("dp")
    core = lax.axis_index("tensor")
    group = lax.axis_index("groups")
    place = ring_place(me, dp_count)
    right = ring_index((place + 1) % dp_count, dp_count)
    left = ring_index((place + dp_count - 1) % dp_count, dp_count)
    other_core = 1 - core
    other_group = 1 - group

    barrier = pltpu.get_barrier_semaphore()
    for k in range(1, dp_count):
        pl.semaphore_signal(barrier, inc=1, device_id={"dp": (me + k) % dp_count}, device_id_type=MESH)
    pl.semaphore_signal(barrier, inc=1, device_id={"tensor": other_core}, device_id_type=MESH)
    pl.semaphore_signal(barrier, inc=1, device_id={"groups": other_group}, device_id_type=MESH)
    pl.semaphore_wait(barrier, dp_count + 1)

    def block(slot):
        return tok_buf.at[pl.ds(slot * rows, rows)]

    def plan(src, dst, sem, axis, target, sends, recvs):
        return pltpu.make_async_remote_copy(
            src_ref=src, dst_ref=dst, send_sem=sends.at[sem], recv_sem=recvs.at[sem],
            device_id={axis: target}, device_id_type=MESH,
        )

    def send(*where):
        copy = plan(*where)
        copy.start()
        return copy

    def inside(place_value):
        return (place_value % half) * (half - 1 - place_value % half) > 0

    across = ring_index(dp_count - 1 - place, dp_count)
    middle = inside(place)
    right_end = jnp.logical_not(inside((place + 1) % dp_count))
    left_end = jnp.logical_not(inside((place + dp_count - 1) % dp_count))

    last = dp_count - 1
    cut = rows // 2
    cw = send(tokens, block(1), 0, "dp", right, ring_send, ring_recv)
    ccw = send(tokens, block(2), 1, "dp", left, ring_send, ring_recv)

    loads = [
        pltpu.make_async_copy(tokens, block(0), load_sem.at[0]),
        pltpu.make_async_copy(gate, weights.at[0], load_sem.at[1]),
        pltpu.make_async_copy(up, weights.at[1], load_sem.at[2]),
        pltpu.make_async_copy(down, down_buf, load_sem.at[3]),
    ]
    for load in loads:
        load.start()

    share = ranks // group_count
    mine = pl.ds(pl.multiple_of(group * share, 16), share)
    landing = pl.ds(pl.multiple_of(core * ranks + group * share, 16), share)
    ad_copies = []
    for k in range(1, dp_count):
        target = (me + k) % dp_count
        ad_copies.append(send(
            adapter_up.at[mine, pl.ds(pl.multiple_of(target * units, 128), units)],
            adapters_out.at[me, landing], k, "dp", target, ad_send, ad_recv,
        ))
    ad_local = pltpu.make_async_copy(
        adapter_up.at[mine, pl.ds(pl.multiple_of(me * units, 128), units)],
        adapters_out.at[me, landing], load_sem.at[4],
    )
    ad_local.start()
    for load in loads:
        load.wait()

    def project(slot, blocks, matrices=(0, 2)):
        def chunk(step, carry):
            which = step // (units // unit_chunk)
            first = pl.multiple_of((step % (units // unit_chunk)) * unit_chunk, unit_chunk)
            value = lax.dot_general(
                weights[which, pl.ds(first, unit_chunk), :],
                tok_buf[pl.ds(slot * rows, blocks * rows), :],
                (((1,), (1,)), ((), ())), preferred_element_type=jnp.float32,
            )
            for b in range(blocks):
                parts[slot + b, which, pl.ds(first, unit_chunk), :] = value[:, b * rows:(b + 1) * rows]
            return carry

        per_matrix = units // unit_chunk
        lax.fori_loop(matrices[0] * per_matrix, matrices[1] * per_matrix, chunk, 0)

    def project_down(slot, blocks):
        contrib[pl.ds(slot * rows, blocks * rows), :] = jnp.dot(
            tok_buf[pl.ds(slot * rows, blocks * rows), :], down_buf[...],
            preferred_element_type=jnp.float32,
        )
        for j in range(slot, slot + blocks):
            @pl.when(slot_block[j] // per_core != core)
            def _():
                contrib_copy(j).start()

    per_core = dp_count // tp_count
    slot_place = [place]
    for s in range(1, half):
        slot_place += [(place + dp_count - s) % dp_count, (place + s) % dp_count]
    slot_place.append((place + half) % dp_count)
    slot_block = [ring_index(q, dp_count) for q in slot_place]

    def part_copy(slot):
        where = slot_block[slot] % per_core
        return pltpu.make_async_remote_copy(
            src_ref=parts.at[slot], dst_ref=peer_out.at[where],
            send_sem=part_send.at[slot], recv_sem=part_recv.at[where],
            device_id={"tensor": other_core}, device_id_type=MESH,
        )

    def own_copy(slot):
        where = slot_block[slot] % per_core
        return pltpu.make_async_copy(parts.at[slot], own_out.at[where], part_send.at[slot])

    def contrib_copy(slot):
        where = slot_block[slot] % per_core
        return pltpu.make_async_remote_copy(
            src_ref=contrib.at[pl.ds(slot * rows, rows)], dst_ref=contrib_peer.at[where],
            send_sem=con_send.at[slot], recv_sem=con_recv.at[where],
            device_id={"tensor": other_core}, device_id_type=MESH,
        )

    strip = rows // dp_count

    def publish_copy(where, k):
        target = (me + k) % dp_count
        return pltpu.make_async_remote_copy(
            src_ref=published.at[where, pl.ds(pl.multiple_of(target * strip, 16), strip)],
            dst_ref=heard.at[k - 1, where],
            send_sem=pub_send.at[k - 1, where], recv_sem=pub_recv.at[k - 1, where],
            device_id={"dp": (me + k) % dp_count}, device_id_type=MESH,
        )

    def publish(slot):
        where = slot_block[slot] % per_core

        @pl.when(slot_block[slot] // per_core == core)
        def _():
            contrib_copy(slot).wait_recv()
            total = contrib[pl.ds(slot * rows, rows), :] + contrib_peer[where]
            published[where] = (total * owned[slot_block[slot], 0:1, :]).astype(published.dtype)
            for k in range(1, dp_count):
                publish_copy(where, k).start()

    def hand_over(slot):
        @pl.when(slot_block[slot] // per_core == core)
        def _():
            own_copy(slot).start()

        @pl.when(slot_block[slot] // per_core != core)
        def _():
            part_copy(slot).start()

    project_down(0, 1)
    project(0, 1)
    hand_over(0)
    publish(0)
    sent = [cw, ccw]
    passes = []
    for s in range(1, half):
        cw.wait_recv()
        if s < half - 1:
            before = ccw
            cw = send(block(2 * s - 1), block(2 * s + 1), 2 * s, "dp", right, ring_send, ring_recv)
            before.wait_recv()
            ccw = send(block(2 * s), block(2 * s + 2), 2 * s + 1, "dp", left, ring_send, ring_recv)
        else:
            a, b = (2 * s - 1) * rows, 2 * s * rows + cut
            z = last * rows
            last_cw = plan(tok_buf.at[pl.ds(a, cut)], tok_buf.at[pl.ds(z, cut)],
                           2 * s, "dp", right, ring_send, ring_recv)
            last_ccw = plan(tok_buf.at[pl.ds(b, cut)], tok_buf.at[pl.ds(z + cut, cut)],
                            2 * s + 1, "dp", left, ring_send, ring_recv)
            pl.when(right_end)(last_cw.start)
            ccw.wait_recv()
            pl.when(left_end)(last_ccw.start)
        if s < half - 1:
            sent += [cw, ccw]
        if s == 1:
            source = pl.multiple_of((1 + place % 2) * rows, rows)
            crossing = plan(tok_buf.at[pl.ds(source, rows)], block(last),
                            0, "dp", across, cross_send, cross_recv)
            pl.when(middle)(crossing.start)
        project_down(2 * s - 1, 2)
        project(2 * s - 1, 2)
        hand_over(2 * s - 1)
        hand_over(2 * s)
        publish(2 * s - 1)
        publish(2 * s)
        if s == half - 2:
            for copy in ad_copies:
                copy.wait_recv()
            ad_local.wait()
            region = adapters_out.at[:, landing]
            passes.append(send(region, region, 0, "groups", other_group, pass_send, pass_recv))
        if s == half - 1:
            passes[0].wait_recv()
            region = adapters_out.at[:, pl.ds(pl.multiple_of(core * ranks, 16), ranks)]
            passes.append(send(region, region, 1, "tensor", other_core, pass_send, pass_recv))

    @pl.when(middle)
    def _():
        crossing.wait_recv()
        crossing.wait_send()

    @pl.when(jnp.logical_not(middle))
    def _():
        last_cw.wait_recv()
        last_ccw.wait_recv()

    project_down(last, 1)
    publish(last)
    project(last, 1, (0, 1))
    for where in range(per_core):
        for k in range(1, dp_count):
            publish_copy(where, k).wait_recv()
        total = published[where, pl.ds(pl.multiple_of(me * strip, 16), strip), :].astype(jnp.float32)
        for k in range(1, dp_count):
            total = total + heard[k - 1, where].astype(jnp.float32)
        reduced[where] = total.astype(reduced.dtype)
    spreads = []
    for k in range(1, dp_count):
        spreads.append(send(
            reduced, gathered.at[me], k, "dp", (me + k) % dp_count, red_send, red_recv
        ))
    project(last, 1, (1, 2))
    hand_over(last)
    for copy in spreads:
        copy.wait_recv()
    gathered[me] = reduced[...]
    for where in range(per_core):
        for d in range(dp_count):
            down_out[pl.ds(where * rows + d * strip, strip), :] = gathered[d, where]

    pl.when(right_end)(last_cw.wait_send)
    pl.when(left_end)(last_ccw.wait_send)
    for copy in sent + ad_copies + passes + spreads:
        copy.wait_send()
    passes[1].wait_recv()
    for slot in range(dp_count):
        @pl.when(slot_block[slot] // per_core == core)
        def _():
            own_copy(slot).wait()

        @pl.when(slot_block[slot] // per_core != core)
        def _():
            part_copy(slot).wait_send()
            contrib_copy(slot).wait_send()

    for where in range(per_core):
        for k in range(1, dp_count):
            publish_copy(where, k).wait_send()
        pltpu.make_async_remote_copy(
            src_ref=parts.at[where], dst_ref=peer_out.at[where],
            send_sem=part_send.at[where], recv_sem=part_recv.at[where],
            device_id={"tensor": other_core}, device_id_type=MESH,
        ).wait_recv()


def finish(ids, own, peer, adapters, down_proj, ref_out, pol_out, sums):
    blocks = own.shape[0]
    rows = own.shape[3]
    ranks = down_proj.shape[1] // 2

    @pl.when(pl.program_id(0) == 0)
    def _():
        sums[...] = jnp.zeros_like(sums)

    def silu(v):
        return v / (1.0 + jnp.exp(-v))

    contract = (((0,), (1,)), ((), ()))
    for j in range(blocks):
        columns = slice(j * rows, (j + 1) * rows)
        gate = own[j, 0] + peer[j, 0]
        up = own[j, 1] + peer[j, 1]
        chosen = adapters[ids[j]]
        ref_hidden = (silu(gate) * up).astype(jnp.bfloat16)
        ref_out[:, columns] = ref_hidden
        gate = gate + lax.dot_general(
            chosen[:ranks], down_proj[columns, :ranks], contract, preferred_element_type=jnp.float32
        )
        up = up + lax.dot_general(
            chosen[ranks:], down_proj[columns, ranks:], contract, preferred_element_type=jnp.float32
        )
        pol_hidden = (silu(gate) * up).astype(jnp.bfloat16)
        pol_out[:, columns] = pol_hidden
        ref_vals = 4.0 * jnp.tanh(ref_hidden.astype(jnp.float32) * 0.25)
        pol_vals = 4.0 * jnp.tanh(pol_hidden.astype(jnp.float32) * 0.25)
        pol_exp = jnp.exp(pol_vals)
        for k, value in enumerate((jnp.exp(ref_vals), pol_exp, pol_exp * (pol_vals - ref_vals))):
            sums[k, :, columns] += value.reshape(-1, 8, rows).sum(axis=0)


def divergence(dp_count, sums, live, out, mine, heard, halves, send_sem, recv_sem):
    me = lax.axis_index("dp")
    other_core = 1 - lax.axis_index("tensor")
    barrier = pltpu.get_barrier_semaphore()
    for k in range(1, dp_count):
        pl.semaphore_signal(barrier, inc=1, device_id={"dp": (me + k) % dp_count}, device_id_type=MESH)
    pl.semaphore_signal(barrier, inc=1, device_id={"tensor": other_core}, device_id_type=MESH)
    for k in range(3):
        mine[k:k + 1, :] = jnp.sum(sums[k], axis=0, keepdims=True)
    mine[3:8, :] = jnp.zeros((5, mine.shape[1]), jnp.float32)
    pl.semaphore_wait(barrier, dp_count)
    copies = []
    for k in range(1, dp_count):
        copies.append(pltpu.make_async_remote_copy(
            src_ref=mine, dst_ref=heard.at[me], send_sem=send_sem.at[k], recv_sem=recv_sem.at[k],
            device_id={"dp": (me + k) % dp_count}, device_id_type=MESH,
        ))
        copies[-1].start()
    for copy in copies:
        copy.wait_recv()
    heard[me] = mine[...]
    total = heard[0]
    for k in range(1, dp_count):
        total = total + heard[k]
    ref_sum, pol_sum, cross_sum = total[0:1], total[1:2], total[2:3]
    kl_row = cross_sum / pol_sum - jnp.log(pol_sum) + jnp.log(ref_sum)
    part = jnp.sum(live[...] * kl_row, axis=1, keepdims=True)
    halves[0] = jnp.broadcast_to(part, (8, 128))
    swap = pltpu.make_async_remote_copy(
        src_ref=halves.at[0], dst_ref=halves.at[1], send_sem=send_sem.at[0], recv_sem=recv_sem.at[0],
        device_id={"tensor": other_core}, device_id_type=MESH,
    )
    swap.start()
    swap.wait()
    for copy in copies:
        copy.wait_send()
    out[...] = halves[0] + halves[1]


def kernel_shards(
    tokens, gate_weight_base, up_weight_base, adapter_down_stack, adapter_up_stack,
    segment_block_counts, segment_adapter_ids, segment_live_rows,
):
    dp_count = lax.axis_size("dp")
    tp_count = lax.axis_size("tensor")
    group_count = lax.axis_size("groups")
    dp_index = lax.axis_index("dp")
    tp_index = lax.axis_index("tensor")
    local_rows, features = tokens.shape
    units = gate_weight_base.shape[0]
    ranks = adapter_up_stack.shape[1]
    total_rows = local_rows * dp_count
    per_core = dp_count // tp_count
    rows_half = total_rows // tp_count
    member, live_rows, counts = segment_tables(segment_block_counts, segment_live_rows, total_rows)
    row_adapter = jnp.sum(member.astype(jnp.int32) * segment_adapter_ids[:, None], axis=0)
    f32, bf16 = jnp.float32, jnp.bfloat16
    any_spec = pl.BlockSpec(memory_space=pl.ANY)
    dma = pltpu.SemaphoreType.DMA
    owned = jnp.broadcast_to(
        (row_adapter[::local_rows] == dp_index).astype(f32)[:, None, None],
        (dp_count, 8, tp_count * ranks),
    )
    vmem_spec = pl.BlockSpec(memory_space=pltpu.VMEM)
    own, peer, adapters, own_down = pl.pallas_call(
        functools.partial(gather_project, dp_count, tp_count, group_count, units // 2),
        out_shape=(
            jax.ShapeDtypeStruct((per_core, 2, units, local_rows), f32),
            jax.ShapeDtypeStruct((per_core, 2, units, local_rows), f32),
            jax.ShapeDtypeStruct((dp_count, tp_count * ranks, units), bf16),
            jax.ShapeDtypeStruct((rows_half, tp_count * ranks), bf16),
        ),
        in_specs=[any_spec] * 5 + [vmem_spec],
        out_specs=(any_spec,) * 3 + (vmem_spec,),
        scratch_shapes=[
            pltpu.VMEM((total_rows, features), bf16),
            pltpu.VMEM((2, units, features), bf16),
            pltpu.VMEM((features, tp_count * ranks), bf16),
            pltpu.VMEM((dp_count, 2, units, local_rows), f32),
            pltpu.VMEM((total_rows, tp_count * ranks), f32),
            pltpu.VMEM((per_core, local_rows, tp_count * ranks), f32),
            pltpu.VMEM((per_core, local_rows, tp_count * ranks), bf16),
            pltpu.VMEM((dp_count - 1, per_core, local_rows // dp_count, tp_count * ranks), bf16),
            pltpu.VMEM((per_core, local_rows // dp_count, tp_count * ranks), bf16),
            pltpu.VMEM((dp_count, per_core, local_rows // dp_count, tp_count * ranks), bf16),
            dma((5,)), dma((dp_count,)), dma((dp_count,)), dma((dp_count,)), dma((dp_count,)),
            dma((2,)), dma((2,)), dma((dp_count,)), dma((per_core,)), dma((dp_count,)), dma((per_core,)),
            dma((dp_count - 1, per_core)), dma((dp_count - 1, per_core)), dma((dp_count,)), dma((dp_count,)),
            dma((1,)), dma((1,)),
        ],
        compiler_params=pltpu.CompilerParams(
            collective_id=0, has_side_effects=True, vmem_limit_bytes=60 * 1024 * 1024
        ),
        name="gather_project",
    )(tokens, gate_weight_base, up_weight_base, adapter_down_stack[0], adapter_up_stack[0], owned)
    own_ids = lax.dynamic_slice_in_dim(row_adapter[::local_rows], tp_index * per_core, per_core, 0)
    chunk = 256
    ref_hidden, pol_hidden, sums = pl.pallas_call(
        finish,
        out_shape=(
            jax.ShapeDtypeStruct((units, rows_half), bf16),
            jax.ShapeDtypeStruct((units, rows_half), bf16),
            jax.ShapeDtypeStruct((3, 8, rows_half), f32),
        ),
        grid_spec=pltpu.PrefetchScalarGridSpec(
            num_scalar_prefetch=1,
            grid=(units // chunk,),
            in_specs=[
                pl.BlockSpec((per_core, 2, chunk, local_rows), lambda u, ids: (0, 0, u, 0)),
                pl.BlockSpec((per_core, 2, chunk, local_rows), lambda u, ids: (0, 0, u, 0)),
                pl.BlockSpec((dp_count, tp_count * ranks, chunk), lambda u, ids: (0, 0, u)),
                pl.BlockSpec((rows_half, tp_count * ranks), lambda u, ids: (0, 0)),
            ],
            out_specs=[
                pl.BlockSpec((chunk, rows_half), lambda u, ids: (u, 0)),
                pl.BlockSpec((chunk, rows_half), lambda u, ids: (u, 0)),
                pl.BlockSpec((3, 8, rows_half), lambda u, ids: (0, 0, 0)),
            ],
        ),
        compiler_params=pltpu.CompilerParams(vmem_limit_bytes=60 * 1024 * 1024),
        name="finish",
    )(own_ids, own, peer, adapters, own_down)
    seg_count = live_rows.shape[0]
    spread = jnp.zeros((8, total_rows), f32).at[:seg_count].set(live_rows.astype(f32))
    own_live = lax.dynamic_slice_in_dim(spread, tp_index * rows_half, rows_half, 1)
    seg_sums = pl.pallas_call(
        functools.partial(divergence, dp_count),
        out_shape=jax.ShapeDtypeStruct((8, 128), f32),
        in_specs=[vmem_spec] * 2,
        out_specs=vmem_spec,
        scratch_shapes=[
            pltpu.VMEM((8, rows_half), f32),
            pltpu.VMEM((dp_count, 8, rows_half), f32),
            pltpu.VMEM((2, 8, 128), f32),
            dma((dp_count,)), dma((dp_count,)),
        ],
        compiler_params=pltpu.CompilerParams(collective_id=1, has_side_effects=True),
        name="divergence",
    )(sums, own_live)
    seg_kl = seg_sums[:seg_count, 0] / counts
    return (ref_hidden, pol_hidden, seg_kl)


def pick_shards(*args):
    rows = args[0].shape[0]
    units = args[1].shape[0]
    sizes = (lax.axis_size("groups"), lax.axis_size("tensor"))
    fits = rows == BLOCK and units % 256 == 0 and sizes == (2, 2) and lax.axis_size("dp") == 8
    return kernel_shards(*args) if fits else shards(*args)


def solution(mesh):
    in_specs = (
        P(("groups", "dp"), "tensor"),
        P("dp", "tensor"),
        P("dp", "tensor"),
        P("dp", "tensor", None),
        P("dp", "tensor", None),
        P("groups"),
        P("groups"),
        P("groups"),
    )
    out_specs = (P("dp", ("groups", "tensor")), P("dp", ("groups", "tensor")), P("groups"))
    return jax.shard_map(pick_shards, mesh=mesh, in_specs=in_specs, out_specs=out_specs, check_vma=False)
```
